128 devices in a mesh: lat: 8 (over x, z_lo), lon: 16 (over z_hi, y, core).
Axes of the slice: x: 4, y: 4, z: 4 (z_hi: 2, z_lo: 2; z = z_hi * 2 + z_lo), core: 2. Of those that a mesh axis runs over, the one named last changes fastest.
Arguments:
- gridded_observations: bfloat16 [256, 768, 72], P('lat', 'lon'), may hold values from -6 to 6
- footprint_offsets: int32 [128, 32], replicated, may hold values from 0 to 59, as said below
- coarsening_kernel_entries: bfloat16 [128, 9, 32], replicated, may hold values from -1 to 1
- coarsening_matrix: bfloat16 [648, 512], replicated, may hold values from -0.25 to 0.25
- coarsening_offset: float32 [512], replicated, may hold values from -3 to 3
- first_norm_scale: float32 [512], replicated, may hold values from 0.1 to 1.9
- neighbourhood_kernel_entries: bfloat16 [128, 9, 21], P('lat'), may hold values from -1.25 to 1.25
- polar_kernel_entries: bfloat16 [2, 3, 9, 3, 384], replicated, may hold values from -0.1875 to 0.1875
- mixing_matrix: bfloat16 [4608, 512], replicated, may hold values from -0.09375 to 0.09375
- second_norm_scale: float32 [512], replicated, may hold values from 0.1 to 1.9
- expansion_matrix: bfloat16 [512, 1024], replicated, may hold values from -0.25 to 0.25
- expansion_offset: float32 [1024], replicated, may hold values from -3 to 3
- contraction_matrix: bfloat16 [1024, 512], replicated, may hold values from -0.1875 to 0.1875
Outputs:
- encoded: bfloat16 [128, 384, 512], P('lat', 'lon')
The draws below stay inside these ranges and needn't reach their ends.
Inputs may be any that keep to these rules, and one draw needn't show every extreme that they name: `footprint_offsets`: in every cycle the 32 entries of support are distinct cells of the 6 x 10 window.
All inputs are finite; a program needn't handle non-finite values.
Results may differ from the reference program's by a relative error of at most 0.018.
Values may be sent and summed in bfloat16 or wider, within the bound.
A program may use at most 128 MiB of HBM per device.

```python
import jax
import jax.numpy as jnp
from jax import lax

PHYSICAL_FIELDS = 72
FEATURE_WIDTH = 512
HID = 1024
KERNEL_FAMILY = 9
RIN = 6
LWIN = 10
FOOTPRINT_CELLS = 32
RLOC = 3
LLOC = 7
CAPR = 3
SHARD_PARALLELS = 16
COARSE_PARALLELS = 128
COARSE_MERIDIANS = 384
NLAT_IN = 256
NLON_IN = 768
N_LAT = 8


def draw_footprint_offsets(key, part):
    key = jax.random.fold_in(key, 11)
    window_cells = RIN * LWIN
    scores = jax.random.randint(key, (COARSE_PARALLELS, window_cells), 0, 1 << 20) * 64 + jnp.arange(window_cells, dtype=jnp.int32)[None, :]
    order = jnp.argsort(scores, axis=1, stable=True)
    return order[:, :FOOTPRINT_CELLS].astype(jnp.int32)


def level_of(rng, dims, shards, low, high):
    loudness = 1.0
    for axis_at, blocks in shards:
        heights = jax.random.uniform(jax.random.fold_in(jax.random.fold_in(rng, 6), axis_at), (blocks,), jnp.float32, low / len(shards), high / len(shards))
        loudness = loudness * jnp.repeat(jnp.exp(heights), dims[axis_at] // blocks).reshape((-1,) + (1,) * (len(dims) - 1 - axis_at))
    return loudness


def centred(key, dims, scale, limit, split=(), kind=jnp.bfloat16):
    drawn = jax.random.normal(key, dims, jnp.float32) * scale
    if len(split) > 0:
        drawn = level_of(key, dims, split, -0.22, 0.18) * drawn
    return jnp.clip(drawn, min=-limit, max=limit).astype(kind)


def setup_inputs(seed: int = 0) -> dict:
    keys = jax.random.split(jax.random.key(seed), 14)
    gridded_observations = centred(keys[0], (NLAT_IN, NLON_IN, PHYSICAL_FIELDS), 1.0, 6.0, ((0, 8), (1, 16)))
    footprint_offsets = draw_footprint_offsets(jax.random.fold_in(keys[13], 71), 0)
    coarsening_kernel_entries = centred(keys[2], (COARSE_PARALLELS, KERNEL_FAMILY, FOOTPRINT_CELLS), FOOTPRINT_CELLS ** -0.5, 1.0)
    coarsening_matrix = centred(keys[3], (KERNEL_FAMILY * PHYSICAL_FIELDS, FEATURE_WIDTH), (KERNEL_FAMILY * PHYSICAL_FIELDS) ** -0.5, 0.25)
    coarsening_offset = centred(keys[4], (FEATURE_WIDTH,), 0.5, 3.0, (), jnp.float32)
    first_norm_scale = jnp.clip(1.0 + 0.18 * jax.random.normal(keys[5], (FEATURE_WIDTH,), jnp.float32), 0.1, 1.9)
    neighbourhood_kernel_entries = centred(keys[6], (COARSE_PARALLELS, KERNEL_FAMILY, RLOC * LLOC), (RLOC * LLOC) ** -0.5, 1.25, ((0, 8),))
    polar_kernel_entries = centred(keys[7], (2, CAPR, KERNEL_FAMILY, RLOC, COARSE_MERIDIANS), (RLOC * COARSE_MERIDIANS) ** -0.5, 0.1875)
    mixing_matrix = centred(keys[8], (KERNEL_FAMILY * FEATURE_WIDTH, FEATURE_WIDTH), (KERNEL_FAMILY * FEATURE_WIDTH) ** -0.5, 0.09375)
    second_norm_scale = jnp.clip(1.0 + 0.18 * jax.random.normal(keys[9], (FEATURE_WIDTH,), jnp.float32), 0.1, 1.9)
    expansion_matrix = centred(keys[10], (FEATURE_WIDTH, HID), FEATURE_WIDTH ** -0.5, 0.25)
    expansion_offset = centred(keys[11], (HID,), 0.5, 3.0, (), jnp.float32)
    contraction_matrix = centred(keys[12], (HID, FEATURE_WIDTH), HID ** -0.5, 0.1875)
    return dict(gridded_observations=gridded_observations, footprint_offsets=footprint_offsets, coarsening_kernel_entries=coarsening_kernel_entries, coarsening_matrix=coarsening_matrix, coarsening_offset=coarsening_offset, first_norm_scale=first_norm_scale, neighbourhood_kernel_entries=neighbourhood_kernel_entries, polar_kernel_entries=polar_kernel_entries, mixing_matrix=mixing_matrix, second_norm_scale=second_norm_scale, expansion_matrix=expansion_matrix, expansion_offset=expansion_offset, contraction_matrix=contraction_matrix)


norm_epsilon = 1e-05

def layer_norm(inputs, gain):
    wide = inputs.astype(jnp.float32)
    center = lax.optimization_barrier(jnp.mean(wide, axis=-1, keepdims=True))
    spread = lax.optimization_barrier(jnp.mean(jnp.square(wide - center), axis=-1, keepdims=True))
    return ((wide - center) * lax.rsqrt(spread + norm_epsilon) * gain).astype(jnp.bfloat16)

def circulant(psi_cycle, offsets, length):
    doubled = jnp.concatenate([psi_cycle, psi_cycle], axis=-1)
    return jax.vmap(lambda offset: lax.dynamic_slice_in_dim(doubled, offset, length, axis=2))(offsets)

def coarsen_sphere(haloed_source, footprint_parts, kernel_entry_stack, coarsening_matrix, coarsening_offset, parallel_index, meridian_count):
    window_cells = RIN * LWIN
    onehot = (footprint_parts[:, :, None] == jnp.arange(window_cells, dtype=jnp.int32)[None, None, :]).astype(jnp.float32)
    dense_filter = jnp.einsum('iks,isc->ikc', kernel_entry_stack.astype(jnp.float32), onehot).astype(jnp.bfloat16)
    dense_filter = dense_filter.reshape(parallel_index, KERNEL_FAMILY, RIN, LWIN)
    columns = jnp.stack([haloed_source[:, col_off:col_off + 2 * meridian_count - 1:2] for col_off in range(LWIN)], axis=2)
    accumulated = jnp.zeros((parallel_index, meridian_count, KERNEL_FAMILY, PHYSICAL_FIELDS), jnp.float32)
    for row_off in range(RIN):
        row_slab = columns[row_off:row_off + 2 * parallel_index - 1:2]
        accumulated = accumulated + jnp.einsum('akc,abcv->abkv', dense_filter[:, :, row_off, :].astype(jnp.float32), row_slab.astype(jnp.float32))
    collected_neighbours = accumulated.astype(jnp.bfloat16).reshape(parallel_index * meridian_count, KERNEL_FAMILY * PHYSICAL_FIELDS)
    coarse_features = jnp.dot(collected_neighbours, coarsening_matrix, preferred_element_type=jnp.float32) + coarsening_offset
    return coarse_features.astype(jnp.bfloat16).reshape(parallel_index, meridian_count, FEATURE_WIDTH)

def local_filter(padded_mid, kernel_entry_stack, parallel_index, meridian_count):
    columns = jnp.stack([padded_mid[:, shift_off:shift_off + meridian_count] for shift_off in range(LLOC)], axis=2)
    accumulated = jnp.zeros((parallel_index, meridian_count, KERNEL_FAMILY, FEATURE_WIDTH), jnp.float32)
    for row_off in range(RLOC):
        accumulated = accumulated + jnp.einsum('akd,abdc->abkc', kernel_entry_stack[:, :, row_off * LLOC:(row_off + 1) * LLOC].astype(jnp.float32), columns[row_off:row_off + parallel_index].astype(jnp.float32))
    return accumulated

def cap_cycles(edge_rows, psi_half, north_side):
    zero_row = jnp.zeros((1,) + edge_rows.shape[1:], jnp.bfloat16)
    if north_side:
        padded = jnp.concatenate([zero_row, edge_rows], axis=0)
    else:
        padded = jnp.concatenate([edge_rows, zero_row], axis=0)
    cycle_length = edge_rows.shape[1]
    offsets = (-jnp.arange(cycle_length, dtype=jnp.int32) % cycle_length).astype(jnp.int32)
    cycle_parts = []
    for cycle_slot in range(CAPR):
        kernel = circulant(psi_half[cycle_slot], offsets, cycle_length)
        cycle_parts.append(jnp.einsum('jkrl,rlc->jkc', kernel.astype(jnp.float32), padded[cycle_slot:cycle_slot + RLOC].astype(jnp.float32)))
    return jnp.stack(cycle_parts, axis=0)

def reference(gridded_observations, footprint_offsets, coarsening_kernel_entries, coarsening_matrix, coarsening_offset, first_norm_scale, neighbourhood_kernel_entries, polar_kernel_entries, mixing_matrix, second_norm_scale, expansion_matrix, expansion_offset, contraction_matrix):
    haloed_source = jnp.pad(gridded_observations, ((2, 2), (0, 0), (0, 0)))
    haloed_source = jnp.concatenate([haloed_source[:, -4:], haloed_source, haloed_source[:, :4]], axis=1)
    coarse_shard_parts = []
    for block_index in range(N_LAT):
        starting_parallel = block_index * SHARD_PARALLELS
        coarse_shard_parts.append(coarsen_sphere(haloed_source[2 * starting_parallel:2 * starting_parallel + 2 * SHARD_PARALLELS + 4], footprint_offsets[starting_parallel:starting_parallel + SHARD_PARALLELS], coarsening_kernel_entries[starting_parallel:starting_parallel + SHARD_PARALLELS], coarsening_matrix, coarsening_offset, SHARD_PARALLELS, COARSE_MERIDIANS))
    coarse_features = jnp.concatenate(coarse_shard_parts, axis=0)
    normed = layer_norm(coarse_features, first_norm_scale)
    padded_mid = jnp.pad(normed, ((1, 1), (0, 0), (0, 0)))
    padded_mid = jnp.concatenate([padded_mid[:, -3:], padded_mid, padded_mid[:, :3]], axis=1)
    cap_north = cap_cycles(normed[:CAPR + 1], polar_kernel_entries[0], True)
    cap_south = cap_cycles(normed[COARSE_PARALLELS - CAPR - 1:], polar_kernel_entries[1], False)
    outputs = []
    for block_index in range(N_LAT):
        starting_parallel = block_index * SHARD_PARALLELS
        accumulated = local_filter(padded_mid[starting_parallel:starting_parallel + SHARD_PARALLELS + 2], neighbourhood_kernel_entries[starting_parallel:starting_parallel + SHARD_PARALLELS], SHARD_PARALLELS, COARSE_MERIDIANS)
        if block_index == 0:
            accumulated = accumulated.at[:CAPR].add(cap_north)
        if block_index == N_LAT - 1:
            accumulated = accumulated.at[SHARD_PARALLELS - CAPR:].add(cap_south)
        filtered = accumulated.astype(jnp.bfloat16).reshape(SHARD_PARALLELS * COARSE_MERIDIANS, KERNEL_FAMILY * FEATURE_WIDTH)
        residual = coarse_features[starting_parallel:starting_parallel + SHARD_PARALLELS].reshape(SHARD_PARALLELS * COARSE_MERIDIANS, FEATURE_WIDTH)
        middle = (residual.astype(jnp.float32) + jnp.dot(filtered, mixing_matrix, preferred_element_type=jnp.float32)).astype(jnp.bfloat16)
        normed_two = layer_norm(middle, second_norm_scale)
        hidden = jax.nn.gelu(jnp.dot(normed_two, expansion_matrix, preferred_element_type=jnp.float32) + expansion_offset, approximate=True).astype(jnp.bfloat16)
        encoded = (middle.astype(jnp.float32) + jnp.dot(hidden, contraction_matrix, preferred_element_type=jnp.float32)).astype(jnp.bfloat16)
        outputs.append(encoded.reshape(SHARD_PARALLELS, COARSE_MERIDIANS, FEATURE_WIDTH))
    return jnp.concatenate(outputs, axis=0)
```

```python
import functools

import jax
import jax.numpy as jnp
from jax import lax
from jax.experimental import pallas as pl
from jax.experimental.pallas import tpu as pltpu
from jax.sharding import PartitionSpec as P

VARS = 72
FEAT = 512
HIDDEN = 1024
BASIS = 9
RIN = 6
LWIN = 10
CELLS = 32
RLOC = 3
LLOC = 7
CAP = 3
ROWS = 16
COLS = 24
IN_ROWS = 2 * ROWS
IN_COLS = 2 * COLS
EDGE_ROWS = 4
EDGE_COLS = 16
WIDE = EDGE_COLS + IN_COLS + EDGE_COLS
TALL = EDGE_ROWS + IN_ROWS + EDGE_ROWS
EXT_ROWS = ROWS + 2
EXT_COLS = 32
BATCH = 6
SLOT = 4 * COLS
EPS = 1e-05
bf16, f32 = jnp.bfloat16, jnp.float32
MESH = pl.DeviceIdType.MESH

NEAR = [(0, -1), (0, 1), (-1, 0), (1, 0), (-1, -1), (-1, 1), (1, -1), (1, 1)]
FROM_ROWS = {-1: (0, EDGE_ROWS), 0: (0, IN_ROWS), 1: (IN_ROWS - EDGE_ROWS, EDGE_ROWS)}
TO_ROWS = {-1: EDGE_ROWS + IN_ROWS, 0: EDGE_ROWS, 1: 0}
FROM_COLS = {-1: (0, EDGE_COLS), 0: (0, IN_COLS), 1: (IN_COLS - EDGE_COLS, EDGE_COLS)}
TO_COLS = {-1: EDGE_COLS + IN_COLS, 0: EDGE_COLS, 1: 0}


def norm(wide, gain):
    center = jnp.mean(wide, axis=-1, keepdims=True)
    off = wide - center
    spread = jnp.mean(off * off, axis=-1, keepdims=True)
    return off * lax.rsqrt(spread + EPS) * gain


def gelu(u):
    return 0.5 * u * (1.0 + jnp.tanh(0.7978845608 * (u + 0.044715 * (u * u * u))))


def toeplitz(row, count, shift, stride):
    return pltpu.roll(
        jnp.broadcast_to(row, (count, row.shape[1])), shift, 1, stride=stride, stride_axis=0
    )


def kernel(
    nlat, nlon,
    x, foot, cke, cmat, coff, g1, nk, pol, mix, g2, emat, eoff, kmat,
    out,
    xe, footv, ckev, cmv, coffv, g1v, nkv, polv, mixv, g2v, ematv, eoffv, kmatv,
    entv, tapv, polf, poltaps, cmp, w, b, nv, lat, filt, gath, lhs, pres,
    local_sem, near_send, near_recv, cap_send, cap_recv,
):
    la, lo = lax.axis_index("lat"), lax.axis_index("lon")
    north = la == 0
    south = la == nlat - 1
    polar = north | south
    total = nlat * ROWS

    barrier = pltpu.get_barrier_semaphore()

    def there(dy):
        return (la + dy >= 0) & (la + dy < nlat)

    def greet(dy, dx):
        pl.semaphore_signal(
            barrier, inc=1, device_id=(la + dy, lax.rem(lo + dx + nlon, nlon)), device_id_type=MESH
        )

    for dy in (-1, 1):
        @pl.when(there(dy))
        def _():
            for dx in (-1, 0, 1):
                greet(dy, dx)

    @pl.when(jnp.logical_not(polar))
    def _():
        greet(0, -1)
        greet(0, 1)

    @pl.when(polar)
    def _():
        @pl.loop(1, nlon)
        def _(d):
            greet(0, d)

    pairs = [
        (foot, footv),
        (cke, ckev),
        (nk, nkv),
        (x, xe.at[pl.ds(EDGE_ROWS, IN_ROWS), pl.ds(EDGE_COLS, IN_COLS)]),
        (cmat, cmv),
        (coff, coffv),
        (g1, g1v),
        (pol, polv),
        (g2, g2v),
        (eoff, eoffv),
        (mix, mixv),
        (emat, ematv),
        (kmat, kmatv),
    ]
    FOOT, CKE, NK, OWN, CM, COFF, G1, POL, G2, EOFF, MIX, EMAT, KMAT = range(13)
    local = [pltpu.make_async_copy(s, d, local_sem.at[n]) for n, (s, d) in enumerate(pairs)]
    for copy in local:
        copy.start()

    pl.semaphore_wait(
        barrier,
        jnp.where(polar, nlon - 1, 2) + jnp.where(north, 0, 3) + jnp.where(south, 0, 3),
    )

    def near(n):
        dy, dx = NEAR[n]
        r0, rn = FROM_ROWS[dy]
        c0, cn = FROM_COLS[dx]
        return pltpu.make_async_remote_copy(
            src_ref=x.at[pl.ds(r0, rn), pl.ds(c0, cn)],
            dst_ref=xe.at[pl.ds(TO_ROWS[dy], rn), pl.ds(TO_COLS[dx], cn)],
            send_sem=near_send.at[n],
            recv_sem=near_recv.at[n],
            device_id=(la + dy, lax.rem(lo + dx + nlon, nlon)),
            device_id_type=MESH,
        )

    def each_near(act, sign):
        for dy in (0, -1, 1):
            mine = [n for n in range(8) if NEAR[n][0] == dy]

            def go(mine=mine):
                for n in mine:
                    act(near(n))

            if dy == 0:
                go()
            else:
                pl.when(there(sign * dy))(go)

    each_near(lambda c: c.start(), 1)

    @pl.when(north)
    def _():
        xe[0:EDGE_ROWS] = jnp.zeros((EDGE_ROWS, WIDE, VARS), bf16)

    @pl.when(south)
    def _():
        xe[TALL - EDGE_ROWS : TALL] = jnp.zeros((EDGE_ROWS, WIDE, VARS), bf16)

    nv[EXT_ROWS] = jnp.zeros((EXT_COLS, FEAT), bf16)

    for n in (FOOT, CKE, NK):
        local[n].wait()
    chosen = jnp.where(
        lax.broadcasted_iota(jnp.int32, (EXT_COLS, total), 0) + la * ROWS - 1
        == lax.broadcasted_iota(jnp.int32, (EXT_COLS, total), 1),
        1.0,
        0.0,
    ).astype(bf16)
    for k in range(BASIS):
        entries = lax.dot_general(
            chosen, ckev[k], (((1,), (1,)), ((), ())), preferred_element_type=f32
        )
        entv[:, k, :] = entries[:EXT_ROWS]
    cycle = lax.broadcasted_iota(jnp.int32, (CELLS, total), 1)
    place = lax.broadcasted_iota(jnp.int32, (CELLS, 512), 1).astype(f32)

    @pl.loop(0, EXT_ROWS)
    def _(i):
        cells = footv[...]
        lanes = (cells + (WIDE - LWIN) * ((cells * 205) >> 11) + 6).astype(f32)
        column = jnp.sum(
            jnp.where(cycle == la * ROWS + i - 1, lanes, 0.0), axis=1, keepdims=True
        )
        onehot = jnp.where(column == place, 1.0, 0.0).astype(bf16)
        dense = jnp.dot(entv[i].astype(bf16), onehot, preferred_element_type=f32)
        for k in range(BASIS):
            w[i, k * EXT_COLS : (k + 1) * EXT_COLS, :] = toeplitz(
                dense[k : k + 1], EXT_COLS, 0, 2
            ).astype(bf16)

    s = lax.broadcasted_iota(jnp.int32, (RLOC * LLOC, 128), 0)
    lane = lax.broadcasted_iota(jnp.int32, (RLOC * LLOC, 128), 1)
    spread = jnp.where(
        ((lane & 31) < LLOC) & ((lane >> 5) * LLOC + (lane & 31) == s), 1.0, 0.0
    ).astype(bf16)
    for k in range(BASIS):
        tapv[k] = jnp.dot(nkv[k], spread, preferred_element_type=f32)

    @pl.loop(0, ROWS)
    def _(i):
        b[i] = jnp.concatenate(
            [toeplitz(tapv[k, pl.ds(i, 1), :], COLS, 0, 1) for k in range(BASIS)], axis=0
        ).astype(bf16)

    local[CM].wait()
    for k in range(BASIS):
        cmp[k * 128 : k * 128 + VARS, :] = cmv[k * VARS : (k + 1) * VARS, :]
        cmp[k * 128 + VARS : (k + 1) * 128, :] = jnp.zeros((128 - VARS, FEAT), bf16)

    for n in (COFF, G1, OWN):
        local[n].wait()
    each_near(lambda c: c.wait_recv(), -1)

    first = jnp.where(la < nlat // 2, 1, ROWS - 3)
    offset = coffv[...].reshape(1, FEAT)
    gain = g1v[...].reshape(1, FEAT)

    def cap(d):
        return pltpu.make_async_remote_copy(
            src_ref=gath.at[0],
            dst_ref=gath.at[nlon - d],
            send_sem=cap_send.at[d - 1],
            recv_sem=cap_recv.at[d - 1],
            device_id=(la, lax.rem(lo + d, nlon)),
            device_id_type=MESH,
        )

    @pl.loop(0, EXT_ROWS // BATCH)
    def _(batch):
        parts = []
        for m in range(BATCH):
            i = lax.rem(first + batch * BATCH + m, EXT_ROWS)
            window = xe[pl.ds(2 * i, RIN)].reshape(RIN * WIDE, VARS)
            window = jnp.concatenate(
                [window, jnp.zeros((RIN * WIDE, 128 - VARS), bf16)], axis=1
            )
            window = jnp.concatenate([window, jnp.zeros((512 - RIN * WIDE, 128), bf16)], axis=0)
            got = jnp.dot(w[i], window, preferred_element_type=f32).astype(bf16)
            parts.append(
                jnp.concatenate(
                    [got[k * EXT_COLS : (k + 1) * EXT_COLS] for k in range(BASIS)], axis=1
                )
            )
        latent = jnp.dot(
            jnp.concatenate(parts, axis=0), cmp[...], preferred_element_type=f32
        )
        latent = (latent + offset).astype(bf16).astype(f32)
        normed = norm(latent, gain)
        for m in range(BATCH):
            i = lax.rem(first + batch * BATCH + m, EXT_ROWS)
            g = la * ROWS + i - 1
            lat[i] = latent[m * EXT_COLS : (m + 1) * EXT_COLS]
            row = normed[m * EXT_COLS : (m + 1) * EXT_COLS]
            nv[i] = jnp.where((g >= 0) & (g < total), row, 0.0).astype(bf16)

        @pl.when(polar & (batch == 0))
        def _():
            rows = [
                normed[m * EXT_COLS + 3 : m * EXT_COLS + 3 + COLS] for m in range(4)
            ]
            gath[0] = jnp.concatenate(rows, axis=0).astype(bf16)

            @pl.loop(1, nlon)
            def _(d):
                cap(d).start()

    span = nlon * SLOT

    @pl.when(polar)
    def _():
        local[POL].wait()
        lon_of = lax.broadcasted_iota(jnp.int32, (nlon * COLS, span), 0)
        at = lax.broadcasted_iota(jnp.int32, (nlon * COLS, span), 1)
        dev = at // SLOT
        pick = jnp.where(
            (at - dev * SLOT < COLS) & (dev * COLS + (at - dev * SLOT) == lon_of), 1.0, 0.0
        ).astype(bf16)
        at = lax.broadcasted_iota(jnp.int32, (COLS, span), 1)
        row = lax.broadcasted_iota(jnp.int32, (COLS, span), 0)
        inside = lax.rem(at, COLS) >= row
        cycle = lax.rem(lax.broadcasted_iota(jnp.int32, (1, span), 1), SLOT) // COLS
        lead = jnp.where(north, 1, 0)
        for t in range(CAP):
            for k in range(BASIS):
                for r in range(RLOC):
                    both = polv[t, k, r].astype(f32)
                    n = (t * BASIS + k) * RLOC + r
                    polf[n : n + 1, :] = jnp.where(north, both[0:1], both[1:2])
        poltaps[...] = jnp.dot(polf[...].astype(bf16), pick, preferred_element_type=f32)
        for t in range(CAP):

            @pl.loop(0, BASIS)
            def _(k):
                line = jnp.zeros((1, span), f32)
                for r in range(RLOC):
                    tap = poltaps[pl.ds((t * BASIS + k) * RLOC + r, 1), :]
                    moved = jnp.where(
                        north,
                        pltpu.roll(tap, (COLS * (t + r - 1)) % span, 1),
                        pltpu.roll(tap, COLS * (t + r), 1),
                    )
                    line = line + jnp.where(cycle == t + r - lead, moved, 0.0)
                lhs[t, pl.ds(k * COLS, COLS), :] = jnp.where(
                    inside, toeplitz(line, COLS, 0, 1), toeplitz(line, COLS, SLOT - COLS, 1)
                )

    def filters(i, extra):
        rhs = nv[pl.ds(i, 4)].reshape(4 * EXT_COLS, FEAT)
        got = jnp.dot(b[i], rhs, preferred_element_type=f32)
        return got if extra is None else got + extra

    def filter_pair(i, extra):
        one = filters(i, None if extra is None else pres[extra])
        two = filters(i + 1, None if extra is None else pres[extra + 1])
        for k in range(BASIS):
            both = jnp.concatenate(
                [one[k * COLS : (k + 1) * COLS], two[k * COLS : (k + 1) * COLS]], axis=0
            )
            filt[
                pl.ds(pl.multiple_of(i * COLS, 2 * COLS), 2 * COLS), k * FEAT : (k + 1) * FEAT
            ] = both.astype(bf16)

    expand_offset = eoffv
    gain_two = g2v

    def finish(i, rows):
        at = pl.ds(pl.multiple_of(i * COLS, 4 * COLS), rows * COLS)
        residual = lat[pl.ds(i + 1, rows), 3 : 3 + COLS, :].reshape(rows * COLS, FEAT)
        middle = residual + jnp.dot(filt[at, :], mixv[...], preferred_element_type=f32)
        middle = middle.astype(bf16).astype(f32)
        normed = norm(middle, gain_two[...].reshape(1, FEAT)).astype(bf16)
        hidden = jnp.dot(normed, ematv[...], preferred_element_type=f32)
        hidden = gelu(hidden + expand_offset[...].reshape(1, HIDDEN)).astype(bf16)
        encoded = middle + jnp.dot(hidden, kmatv[...], preferred_element_type=f32)
        out[at, :] = encoded.astype(bf16)

    upper = la < nlat // 2
    big, small = jnp.where(upper, 4, 0), jnp.where(upper, 0, ROWS - 4)

    @pl.loop(0, (ROWS - 4) // 2)
    def _(n):
        filter_pair(big + 2 * n, None)

    for n in (G2, EOFF, MIX, EMAT, KMAT):
        local[n].wait()
    finish(big, ROWS - 4)

    pres[...] = jnp.zeros(pres.shape, f32)

    @pl.when(polar)
    def _():
        @pl.loop(1, nlon)
        def _(d):
            cap(d).wait_recv()

        lead = jnp.where(north, 0, 1)
        everything = gath[...].reshape(span, FEAT)
        for t in range(CAP):
            pres[t + lead] = jnp.dot(
                lhs[t].astype(bf16), everything, preferred_element_type=f32
            )

    filter_pair(small, 0)
    filter_pair(small + 2, 2)
    finish(small, 4)

    each_near(lambda c: c.wait_send(), 1)

    @pl.when(polar)
    def _():
        @pl.loop(1, nlon)
        def _(d):
            cap(d).wait_send()

    @pl.when(jnp.logical_not(polar))
    def _():
        local[POL].wait()


def body(x, foot, cke, cmat, coff, g1, nk, pol, mix, g2, emat, eoff, kmat):
    nlat, nlon = lax.axis_size("lat"), lax.axis_size("lon")
    span = nlon * SLOT
    vmem = pltpu.VMEM
    scratch = [
        vmem((TALL, WIDE, VARS), bf16),
        vmem((CELLS, nlat * ROWS), jnp.int32),
        vmem((BASIS, CELLS, nlat * ROWS), bf16),
        vmem((BASIS * VARS, FEAT), bf16),
        vmem((FEAT,), f32),
        vmem((FEAT,), f32),
        vmem((BASIS, ROWS, RLOC * LLOC), bf16),
        vmem((CAP, BASIS, RLOC, 2, nlon * COLS), bf16),
        vmem((BASIS * FEAT, FEAT), bf16),
        vmem((FEAT,), f32),
        vmem((FEAT, HIDDEN), bf16),
        vmem((HIDDEN,), f32),
        vmem((HIDDEN, FEAT), bf16),
        vmem((EXT_ROWS, BASIS, CELLS), f32),
        vmem((BASIS, ROWS, 128), f32),
        vmem((CAP * BASIS * RLOC, nlon * COLS), f32),
        vmem((CAP * BASIS * RLOC, span), f32),
        vmem((BASIS * 128, FEAT), bf16),
        vmem((EXT_ROWS, BASIS * EXT_COLS, 512), bf16),
        vmem((ROWS, BASIS * COLS, 128), bf16),
        vmem((EXT_ROWS + 1, EXT_COLS, FEAT), bf16),
        vmem((EXT_ROWS, EXT_COLS, FEAT), f32),
        vmem((ROWS * COLS, BASIS * FEAT), bf16),
        vmem((nlon, SLOT, FEAT), bf16),
        vmem((CAP, BASIS * COLS, span), f32),
        vmem((4, BASIS * COLS, FEAT), f32),
        pltpu.SemaphoreType.DMA((13,)),
        pltpu.SemaphoreType.DMA((8,)),
        pltpu.SemaphoreType.DMA((8,)),
        pltpu.SemaphoreType.DMA((nlon - 1,)),
        pltpu.SemaphoreType.DMA((nlon - 1,)),
    ]
    encoded = pl.pallas_call(
        functools.partial(kernel, nlat, nlon),
        out_shape=jax.ShapeDtypeStruct((ROWS * COLS, FEAT), bf16),
        in_specs=[pl.BlockSpec(memory_space=pl.ANY)] * 13,
        out_specs=pl.BlockSpec(memory_space=pltpu.VMEM),
        scratch_shapes=scratch,
        compiler_params=pltpu.CompilerParams(
            collective_id=0, has_side_effects=True, vmem_limit_bytes=56 << 20
        ),
        cost_estimate=pl.CostEstimate(
            flops=3_000_000_000, bytes_accessed=9_000_000, transcendentals=400_000
        ),
    )(
        x,
        foot.T,
        cke.transpose(1, 2, 0),
        cmat,
        coff,
        g1,
        nk.transpose(1, 0, 2),
        pol.transpose(1, 2, 3, 0, 4),
        mix,
        g2,
        emat,
        eoff,
        kmat,
    )
    return encoded.reshape(ROWS, COLS, FEAT)


def solution(mesh):
    return jax.shard_map(
        body,
        mesh=mesh,
        in_specs=(
            P("lat", "lon", None),
            P(),
            P(),
            P(),
            P(),
            P(),
            P("lat", None, None),
            P(),
            P(),
            P(),
            P(),
            P(),
            P(),
        ),
        out_specs=P("lat", "lon", None),
        check_vma=False,
    )
```

```python
import functools

import jax
import jax.numpy as jnp
from jax import lax
from jax.experimental import pallas as pl
from jax.experimental.pallas import tpu as pltpu
from jax.sharding import PartitionSpec as P

VARS = 72
FEAT = 512
HIDDEN = 1024
BASIS = 9
RIN = 6
LWIN = 10
CELLS = 32
RLOC = 3
LLOC = 7
CAP = 3
ROWS = 16
COLS = 24
IN_ROWS = 2 * ROWS
IN_COLS = 2 * COLS
EDGE_ROWS = 4
EDGE_COLS = 16
WIDE = EDGE_COLS + IN_COLS + EDGE_COLS
TALL = EDGE_ROWS + IN_ROWS + EDGE_ROWS
EXT_ROWS = ROWS + 2
EXT_COLS = 32
SLOT = 4 * COLS
EPS = 1e-05
bf16, f32 = jnp.bfloat16, jnp.float32
MESH = pl.DeviceIdType.MESH

HALF = IN_ROWS // 2
NEAR = [(0, -1), (0, 1), (0, -1), (0, 1)] + [(dy, dx) for dy in (-1, 1) for dx in (-1, 0, 1)]
FROM_ROWS = {-1: 0, 1: IN_ROWS - EDGE_ROWS}
TO_ROWS = {-1: EDGE_ROWS + IN_ROWS, 1: 0}
FROM_COLS = {-1: (0, EDGE_COLS), 0: (0, IN_COLS), 1: (IN_COLS - EDGE_COLS, EDGE_COLS)}
TO_COLS = {-1: EDGE_COLS + IN_COLS, 0: EDGE_COLS, 1: 0}
GROUP = 8
WINDOW = 32


def norm(wide, gain):
    center = jnp.mean(wide, axis=-1, keepdims=True)
    off = wide - center
    spread = jnp.mean(off * off, axis=-1, keepdims=True)
    return off * lax.rsqrt(spread + EPS) * gain


def gelu(u):
    return 0.5 * u * (1.0 + jnp.tanh(0.7978845608 * (u + 0.044715 * (u * u * u))))


def toeplitz(row, count, shift, stride):
    return pltpu.roll(
        jnp.broadcast_to(row, (count, row.shape[1])), shift, 1, stride=stride, stride_axis=0
    )


def kernel(
    nlat, nlon,
    x, foot, cke, cmat, coff, g1, nk, pol, mix, g2, emat, eoff, kmat,
    out,
    xe, footv, ckev, cmv, coffv, g1v, nkv, polv, mixv, g2v, ematv, eoffv, kmatv,
    entv, tapv, polf, poltaps, lines, cmp, w, b, nv, lat, filt, gath, lhs, pres,
    local_sem, near_send, near_recv, cap_send, cap_recv, hand_send, hand_recv,
):
    la, lo = lax.axis_index("lat"), lax.axis_index("lon")
    north = la == 0
    south = la == nlat - 1
    polar = north | south
    upper = la < nlat // 2
    total = nlat * ROWS
    chips = nlon // 2
    core = lax.rem(lo, 2)
    sibling = lo + 1 - 2 * core

    barrier = pltpu.get_barrier_semaphore()

    def there(dy):
        return (la + dy >= 0) & (la + dy < nlat)

    def greet(dy, dx):
        pl.semaphore_signal(
            barrier, inc=1, device_id=(la + dy, lax.rem(lo + dx + nlon, nlon)), device_id_type=MESH
        )

    for dy in (-1, 1):
        @pl.when(there(dy))
        def _():
            for dx in (-1, 0, 1):
                greet(dy, dx)

    greet(0, -1)
    greet(0, 1)

    @pl.when(polar)
    def _():
        for m in range(1, chips):
            greet(0, 2 * m)

    pairs = [
        (foot, footv),
        (cke, ckev),
        (nk, nkv),
        (x, xe.at[pl.ds(EDGE_ROWS, IN_ROWS), pl.ds(EDGE_COLS, IN_COLS)]),
        (cmat, cmv),
        (coff, coffv),
        (g1, g1v),
        (pol, polv),
        (g2, g2v),
        (eoff, eoffv),
        (mix, mixv),
        (emat, ematv),
        (kmat, kmatv),
    ]
    FOOT, CKE, NK, OWN, CM, COFF, G1, POL, G2, EOFF, MIX, EMAT, KMAT = range(13)
    local = [pltpu.make_async_copy(s, d, local_sem.at[n]) for n, (s, d) in enumerate(pairs)]
    for n in (FOOT, CKE, NK, OWN):
        local[n].start()

    pl.semaphore_wait(
        barrier,
        2 + jnp.where(polar, chips - 1, 0) + jnp.where(north, 0, 3) + jnp.where(south, 0, 3),
    )

    def near(n):
        dy, dx = NEAR[n]
        c0, cn = FROM_COLS[dx]
        if n < 2:
            r0, rn = jnp.where(upper, 0, HALF), HALF
            to = r0 + EDGE_ROWS
        elif n < 4:
            r0, rn = jnp.where(upper, HALF, 0), HALF
            to = r0 + EDGE_ROWS
        else:
            r0, rn, to = FROM_ROWS[dy], EDGE_ROWS, TO_ROWS[dy]
        return pltpu.make_async_remote_copy(
            src_ref=x.at[pl.ds(r0, rn), pl.ds(c0, cn)],
            dst_ref=xe.at[pl.ds(to, rn), pl.ds(TO_COLS[dx], cn)],
            send_sem=near_send.at[n],
            recv_sem=near_recv.at[n],
            device_id=(la + dy, lax.rem(lo + dx + nlon, nlon)),
            device_id_type=MESH,
        )

    def each_near(act, sign, first, last):
        for n in range(first, min(last, 4)):
            act(near(n))
        if last > 4:
            for dy in (-1, 1):

                @pl.when(there(sign * dy))
                def _():
                    for n in range(4, 10):
                        if NEAR[n][0] == dy:
                            act(near(n))

    each_near(lambda c: c.start(), 1, 0, 10)
    for n in (CM, COFF, G1, POL, G2, EOFF, MIX, EMAT, KMAT):
        local[n].start()

    @pl.when(north)
    def _():
        xe[0:EDGE_ROWS] = jnp.zeros((EDGE_ROWS, WIDE, VARS), bf16)

    @pl.when(south)
    def _():
        xe[TALL - EDGE_ROWS : TALL] = jnp.zeros((EDGE_ROWS, WIDE, VARS), bf16)

    nv[EXT_ROWS] = jnp.zeros((EXT_COLS, FEAT), bf16)

    for n in (FOOT, CKE, NK):
        local[n].wait()
    chosen = jnp.where(
        lax.broadcasted_iota(jnp.int32, (EXT_COLS, total), 0) + la * ROWS - 1
        == lax.broadcasted_iota(jnp.int32, (EXT_COLS, total), 1),
        1.0,
        0.0,
    ).astype(bf16)
    for k in range(BASIS):
        entries = lax.dot_general(
            chosen, ckev[k], (((1,), (1,)), ((), ())), preferred_element_type=f32
        )
        entv[:, k, :] = entries[:EXT_ROWS]
    cycle = lax.broadcasted_iota(jnp.int32, (CELLS, total), 1)
    place = lax.broadcasted_iota(jnp.int32, (CELLS, 256), 1).astype(f32)

    @pl.loop(0, EXT_ROWS)
    def _(i):
        cells = footv[...]
        lanes = (cells + (WINDOW - LWIN) * ((cells * 205) >> 11) + 6).astype(f32)
        column = jnp.sum(
            jnp.where(cycle == la * ROWS + i - 1, lanes, 0.0), axis=1, keepdims=True
        )
        onehot = jnp.where(column == place, 1.0, 0.0).astype(bf16)
        dense = jnp.dot(entv[i].astype(bf16), onehot, preferred_element_type=f32)
        w[i] = jnp.concatenate(
            [toeplitz(dense[k : k + 1], GROUP, 0, 2) for k in range(BASIS)], axis=0
        ).astype(bf16)

    s = lax.broadcasted_iota(jnp.int32, (RLOC * LLOC, 128), 0)
    lane = lax.broadcasted_iota(jnp.int32, (RLOC * LLOC, 128), 1)
    spread = jnp.where(
        ((lane & 31) < LLOC) & ((lane >> 5) * LLOC + (lane & 31) == s), 1.0, 0.0
    ).astype(bf16)
    for k in range(BASIS):
        tapv[k] = jnp.dot(nkv[k], spread, preferred_element_type=f32)

    @pl.loop(0, ROWS)
    def _(i):
        b[i] = jnp.concatenate(
            [toeplitz(tapv[k, pl.ds(i, 1), :], COLS, 0, 1) for k in range(BASIS)], axis=0
        ).astype(bf16)

    local[CM].wait()
    for k in range(BASIS):
        cmp[k * 128 : k * 128 + VARS, :] = cmv[k * VARS : (k + 1) * VARS, :]
        cmp[k * 128 + VARS : (k + 1) * 128, :] = jnp.zeros((128 - VARS, FEAT), bf16)

    for n in (COFF, G1, OWN):
        local[n].wait()

    first = jnp.where(upper, 1, ROWS - 3)
    offset = coffv[...].reshape(1, FEAT)
    gain = g1v[...].reshape(1, FEAT)

    def coarsen(begin, count):
        parts = []
        for m in range(count):
            i = lax.rem(begin + m, EXT_ROWS)
            rows = xe[pl.ds(2 * i, RIN)]
            windows = [
                jnp.concatenate(
                    [
                        rows[:, 16 * a : 16 * a + WINDOW, :].reshape(RIN * WINDOW, VARS),
                        jnp.zeros((RIN * WINDOW, 128 - VARS), bf16),
                    ],
                    axis=1,
                )
                for a in range(EXT_COLS // GROUP)
            ]
            windows = jnp.concatenate(windows, axis=1)
            windows = jnp.concatenate(
                [windows, jnp.zeros((256 - RIN * WINDOW, windows.shape[1]), bf16)], axis=0
            )
            got = jnp.dot(w[i], windows, preferred_element_type=f32)
            for a in range(EXT_COLS // GROUP):
                parts.append(
                    jnp.concatenate(
                        [
                            got[k * GROUP : (k + 1) * GROUP, a * 128 : (a + 1) * 128]
                            for k in range(BASIS)
                        ],
                        axis=1,
                    )
                )
        latent = jnp.dot(
            jnp.concatenate(parts, axis=0).astype(bf16), cmp[...], preferred_element_type=f32
        )
        latent = (latent + offset).astype(bf16).astype(f32)
        normed = norm(latent, gain)
        for m in range(count):
            i = lax.rem(begin + m, EXT_ROWS)
            g = la * ROWS + i - 1
            lat[i] = latent[m * EXT_COLS : (m + 1) * EXT_COLS]
            row = normed[m * EXT_COLS : (m + 1) * EXT_COLS]
            nv[i] = jnp.where((g >= 0) & (g < total), row, 0.0).astype(bf16)
        return normed

    def cap(m):
        return pltpu.make_async_remote_copy(
            src_ref=gath.at[0],
            dst_ref=gath.at[nlon - 2 * m],
            send_sem=cap_send.at[m - 1],
            recv_sem=cap_recv.at[m - 1],
            device_id=(la, lax.rem(lo + 2 * m, nlon)),
            device_id_type=MESH,
        )

    def hand(m, out=True):
        slot = (nlon - 2 * m) % nlon
        west = jnp.where(core == 0, nlon - 1, 1) if out else jnp.where(core == 0, 1, nlon - 1)
        return pltpu.make_async_remote_copy(
            src_ref=gath.at[slot],
            dst_ref=gath.at[lax.rem(slot + west, nlon)],
            send_sem=hand_send.at[m],
            recv_sem=hand_recv.at[m],
            device_id=(la, sibling),
            device_id_type=MESH,
        )

    def pass_on(ms):
        @pl.when(polar)
        def _():
            for m in ms:
                cap(m).wait_recv()
                hand(m).start()

    each_near(lambda c: c.wait_recv(), -1, 0, 2)

    @pl.when(jnp.logical_not(polar))
    def _():
        each_near(lambda c: c.wait_recv(), -1, 2, 10)

    normed = coarsen(first, 4)

    @pl.when(polar)
    def _():
        rows = [normed[m * EXT_COLS + 3 : m * EXT_COLS + 3 + COLS] for m in range(4)]
        gath[0] = jnp.concatenate(rows, axis=0).astype(bf16)
        for m in range(1, chips):
            cap(m).start()
        hand(0).start()
        each_near(lambda c: c.wait_recv(), -1, 2, 10)

    order = sorted(range(1, chips), key=lambda m: (min(m, chips - m), m))
    third = -(-len(order) // 3)

    @pl.loop(0, 2)
    def _(n):
        coarsen(first + 4 + 7 * n, 7)

    span = nlon * SLOT

    @pl.when(polar)
    def _():
        local[POL].wait()
        lane = lax.broadcasted_iota(jnp.int32, (1, span), 1)
        dev = lane // SLOT
        inner = lane - dev * SLOT
        cycle = inner // COLS
        inner = inner - cycle * COLS
        source = jnp.where(cycle == 0, dev * COLS + inner, -1)
        pick = jnp.where(
            lax.broadcasted_iota(jnp.int32, (nlon * COLS, span), 0) == source, 1.0, 0.0
        ).astype(bf16)
        lead = jnp.where(north, 1, 0)
        polf[...] = jnp.zeros(polf.shape, f32)
        for t in range(CAP):
            for r in range(RLOC):
                for k in range(BASIS):
                    both = polv[t, k, r].astype(f32)
                    n = (t * RLOC + r) * 16 + k
                    polf[n : n + 1, :] = jnp.where(north, both[0:1], both[1:2])
        poltaps[...] = jnp.dot(polf[...].astype(bf16), pick, preferred_element_type=f32)
        for t in range(CAP):
            line = jnp.zeros((16, span), f32)
            for r in range(RLOC):
                n = (t * RLOC + r) * 16
                to = t + r - lead
                moved = pltpu.roll(poltaps[n : n + 16, :], lax.rem(COLS * to + span, span), 1)
                line = line + jnp.where(cycle == to, moved, 0.0)
            lines[t * 16 : (t + 1) * 16, :] = line
        inside = inner >= lax.broadcasted_iota(jnp.int32, (COLS, span), 0)

        def circulant(n):
            t = n // BASIS
            line = lines[pl.ds(t * 16 + n - t * BASIS, 1), :]
            return jnp.where(
                inside, toeplitz(line, COLS, 0, 1), toeplitz(line, COLS, SLOT - COLS, 1)
            )

        @pl.loop(0, (CAP * BASIS + 1) // 2)
        def _(n):
            both = jnp.concatenate(
                [circulant(2 * n), circulant(jnp.minimum(2 * n + 1, CAP * BASIS - 1))], axis=0
            )
            lhs[pl.ds(pl.multiple_of(2 * COLS * n, 2 * COLS), 2 * COLS), :] = both.astype(bf16)

    pass_on(order[:third])

    def filters(i, extra):
        rhs = nv[pl.ds(i, 4)].reshape(4 * EXT_COLS, FEAT)
        got = jnp.dot(b[i], rhs, preferred_element_type=f32)
        return got if extra is None else got + extra

    def filter_pair(i, extra):
        one = filters(i, None if extra is None else pres[extra])
        two = filters(i + 1, None if extra is None else pres[extra + 1])
        for k in range(BASIS):
            both = jnp.concatenate(
                [one[k * COLS : (k + 1) * COLS], two[k * COLS : (k + 1) * COLS]], axis=0
            )
            filt[
                pl.ds(pl.multiple_of(i * COLS, 2 * COLS), 2 * COLS), k * FEAT : (k + 1) * FEAT
            ] = both.astype(bf16)

    expand_offset = eoffv
    gain_two = g2v

    def finish(i, rows):
        at = pl.ds(pl.multiple_of(i * COLS, 4 * COLS), rows * COLS)
        residual = lat[pl.ds(i + 1, rows), 3 : 3 + COLS, :].reshape(rows * COLS, FEAT)
        middle = residual + jnp.dot(filt[at, :], mixv[...], preferred_element_type=f32)
        middle = middle.astype(bf16).astype(f32)
        normed = norm(middle, gain_two[...].reshape(1, FEAT)).astype(bf16)
        hidden = jnp.dot(normed, ematv[...], preferred_element_type=f32)
        hidden = gelu(hidden + expand_offset[...].reshape(1, HIDDEN)).astype(bf16)
        encoded = middle + jnp.dot(hidden, kmatv[...], preferred_element_type=f32)
        out[at, :] = encoded.astype(bf16)

    big, small = jnp.where(upper, 4, 0), jnp.where(upper, 0, ROWS - 4)

    @pl.loop(0, (ROWS - 4) // 2)
    def _(n):
        filter_pair(big + 2 * n, None)

    pass_on(order[third : 2 * third])
    for n in (G2, EOFF, MIX, EMAT, KMAT):
        local[n].wait()
    finish(big, ROWS - 4)
    pass_on(order[2 * third :])

    pres[...] = jnp.zeros(pres.shape, f32)

    @pl.when(polar)
    def _():
        for m in range(chips):
            hand(m, False).wait_recv()
        lead = jnp.where(north, 0, 1)
        got = jnp.dot(lhs[...], gath[...].reshape(span, FEAT), preferred_element_type=f32)
        for t in range(CAP):
            pres[t + lead] = got[t * BASIS * COLS : (t + 1) * BASIS * COLS]

    filter_pair(small, 0)
    filter_pair(small + 2, 2)
    finish(small, 4)

    each_near(lambda c: c.wait_send(), 1, 0, 10)

    @pl.when(polar)
    def _():
        for m in range(1, chips):
            cap(m).wait_send()
        for m in range(chips):
            hand(m).wait_send()

    @pl.when(jnp.logical_not(polar))
    def _():
        local[POL].wait()


def body(x, foot, cke, cmat, coff, g1, nk, pol, mix, g2, emat, eoff, kmat):
    nlat, nlon = lax.axis_size("lat"), lax.axis_size("lon")
    span = nlon * SLOT
    vmem = pltpu.VMEM
    scratch = [
        vmem((TALL, WIDE, VARS), bf16),
        vmem((CELLS, nlat * ROWS), jnp.int32),
        vmem((BASIS, CELLS, nlat * ROWS), bf16),
        vmem((BASIS * VARS, FEAT), bf16),
        vmem((FEAT,), f32),
        vmem((FEAT,), f32),
        vmem((BASIS, ROWS, RLOC * LLOC), bf16),
        vmem((CAP, BASIS, RLOC, 2, nlon * COLS), bf16),
        vmem((BASIS * FEAT, FEAT), bf16),
        vmem((FEAT,), f32),
        vmem((FEAT, HIDDEN), bf16),
        vmem((HIDDEN,), f32),
        vmem((HIDDEN, FEAT), bf16),
        vmem((EXT_ROWS, BASIS, CELLS), f32),
        vmem((BASIS, ROWS, 128), f32),
        vmem((CAP * RLOC * 16, nlon * COLS), f32),
        vmem((CAP * RLOC * 16, span), f32),
        vmem((CAP * 16, span), f32),
        vmem((BASIS * 128, FEAT), bf16),
        vmem((EXT_ROWS, BASIS * GROUP, 256), bf16),
        vmem((ROWS, BASIS * COLS, 128), bf16),
        vmem((EXT_ROWS + 1, EXT_COLS, FEAT), bf16),
        vmem((EXT_ROWS, EXT_COLS, FEAT), f32),
        vmem((ROWS * COLS, BASIS * FEAT), bf16),
        vmem((nlon, SLOT, FEAT), bf16),
        vmem(((CAP * BASIS + 1) * COLS, span), bf16),
        vmem((4, BASIS * COLS, FEAT), f32),
        pltpu.SemaphoreType.DMA((13,)),
        pltpu.SemaphoreType.DMA((10,)),
        pltpu.SemaphoreType.DMA((10,)),
        pltpu.SemaphoreType.DMA((nlon // 2 - 1,)),
        pltpu.SemaphoreType.DMA((nlon // 2 - 1,)),
        pltpu.SemaphoreType.DMA((nlon // 2,)),
        pltpu.SemaphoreType.DMA((nlon // 2,)),
    ]
    encoded = pl.pallas_call(
        functools.partial(kernel, nlat, nlon),
        out_shape=jax.ShapeDtypeStruct((ROWS * COLS, FEAT), bf16),
        in_specs=[pl.BlockSpec(memory_space=pl.ANY)] * 13,
        out_specs=pl.BlockSpec(memory_space=pltpu.VMEM),
        scratch_shapes=scratch,
        compiler_params=pltpu.CompilerParams(
            collective_id=0, has_side_effects=True, vmem_limit_bytes=56 << 20
        ),
        cost_estimate=pl.CostEstimate(
            flops=3_000_000_000, bytes_accessed=9_000_000, transcendentals=400_000
        ),
    )(
        x,
        foot.T,
        cke.transpose(1, 2, 0),
        cmat,
        coff,
        g1,
        nk.transpose(1, 0, 2),
        pol.transpose(1, 2, 3, 0, 4),
        mix,
        g2,
        emat,
        eoff,
        kmat,
    )
    return encoded.reshape(ROWS, COLS, FEAT)


def solution(mesh):
    return jax.shard_map(
        body,
        mesh=mesh,
        in_specs=(
            P("lat", "lon", None),
            P(),
            P(),
            P(),
            P(),
            P(),
            P("lat", None, None),
            P(),
            P(),
            P(),
            P(),
            P(),
            P(),
        ),
        out_specs=P("lat", "lon", None),
        check_vma=False,
    )
```

```python
import functools

import jax
import jax.numpy as jnp
from jax import lax
from jax.experimental import pallas as pl
from jax.experimental.pallas import tpu as pltpu
from jax.sharding import PartitionSpec as P

VARS = 72
FEAT = 512
HIDDEN = 1024
BASIS = 9
RIN = 6
LWIN = 10
CELLS = 32
RLOC = 3
LLOC = 7
CAP = 3
ROWS = 16
COLS = 24
IN_ROWS = 2 * ROWS
IN_COLS = 2 * COLS
EDGE_ROWS = 4
EDGE_COLS = 16
WIDE = EDGE_COLS + IN_COLS + EDGE_COLS
TALL = EDGE_ROWS + IN_ROWS + EDGE_ROWS
EXT_ROWS = ROWS + 2
EXT_COLS = 32
SLOT = 4 * COLS
EPS = 1e-05
bf16, f32 = jnp.bfloat16, jnp.float32
MESH = pl.DeviceIdType.MESH

EARLY = 12
NEAR = [(0, -1), (0, 1), (0, -1), (0, 1)] + [(dy, dx) for dy in (-1, 1) for dx in (-1, 0, 1)]
FROM_ROWS = {-1: 0, 1: IN_ROWS - EDGE_ROWS}
TO_ROWS = {-1: EDGE_ROWS + IN_ROWS, 1: 0}
FROM_COLS = {-1: (0, EDGE_COLS), 0: (0, IN_COLS), 1: (IN_COLS - EDGE_COLS, EDGE_COLS)}
TO_COLS = {-1: EDGE_COLS + IN_COLS, 0: EDGE_COLS, 1: 0}
GROUP = 8
WINDOW = 32


def norm(wide, gain):
    center = jnp.mean(wide, axis=-1, keepdims=True)
    off = wide - center
    spread = jnp.mean(off * off, axis=-1, keepdims=True)
    return off * lax.rsqrt(spread + EPS) * gain


def gelu(u):
    return 0.5 * u * (1.0 + jnp.tanh(0.7978845608 * (u + 0.044715 * (u * u * u))))


def toeplitz(row, count, shift, stride):
    return pltpu.roll(
        jnp.broadcast_to(row, (count, row.shape[1])), shift, 1, stride=stride, stride_axis=0
    )


def kernel(
    nlat, nlon,
    x, foot, cke, cmat, coff, g1, nk, pol, mix, g2, emat, eoff, kmat,
    out,
    xe, footv, ckev, cmv, coffv, g1v, nkv, polv, mixv, g2v, ematv, eoffv, kmatv,
    entv, tapv, polf, poltaps, lines, cmp, w, b, nv, lat, filt, gath, lhs, pres, outv,
    local_sem, near_send, near_recv, cap_send, cap_recv, hand_send, hand_recv, out_sem,
):
    la, lo = lax.axis_index("lat"), lax.axis_index("lon")
    north = la == 0
    south = la == nlat - 1
    polar = north | south
    upper = la < nlat // 2
    total = nlat * ROWS
    chips = nlon // 2
    core = lax.rem(lo, 2)
    sibling = lo + 1 - 2 * core

    barrier = pltpu.get_barrier_semaphore()

    def there(dy):
        return (la + dy >= 0) & (la + dy < nlat)

    def greet(dy, dx):
        pl.semaphore_signal(
            barrier, inc=1, device_id=(la + dy, lax.rem(lo + dx + nlon, nlon)), device_id_type=MESH
        )

    for dy in (-1, 1):
        @pl.when(there(dy))
        def _():
            for dx in (-1, 0, 1):
                greet(dy, dx)

    greet(0, -1)
    greet(0, 1)

    @pl.when(polar)
    def _():
        for m in range(1, chips):
            greet(0, 2 * m)

    pairs = [
        (foot, footv),
        (cke, ckev),
        (nk, nkv),
        (x, xe.at[pl.ds(EDGE_ROWS, IN_ROWS), pl.ds(EDGE_COLS, IN_COLS)]),
        (cmat, cmv),
        (coff, coffv),
        (g1, g1v),
        (pol, polv),
        (g2, g2v),
        (eoff, eoffv),
        (mix, mixv),
        (emat, ematv),
        (kmat, kmatv),
    ]
    FOOT, CKE, NK, OWN, CM, COFF, G1, POL, G2, EOFF, MIX, EMAT, KMAT = range(13)
    local = [pltpu.make_async_copy(s, d, local_sem.at[n]) for n, (s, d) in enumerate(pairs)]
    for n in (FOOT, CKE, NK, OWN):
        local[n].start()

    pl.semaphore_wait(
        barrier,
        2 + jnp.where(polar, chips - 1, 0) + jnp.where(north, 0, 3) + jnp.where(south, 0, 3),
    )

    def near(n):
        dy, dx = NEAR[n]
        c0, cn = FROM_COLS[dx]
        if n < 2:
            r0, rn = jnp.where(upper, 0, IN_ROWS - EARLY), EARLY
            to = r0 + EDGE_ROWS
        elif n < 4:
            r0, rn = jnp.where(upper, EARLY, 0), IN_ROWS - EARLY
            to = r0 + EDGE_ROWS
        else:
            r0, rn, to = FROM_ROWS[dy], EDGE_ROWS, TO_ROWS[dy]
        return pltpu.make_async_remote_copy(
            src_ref=x.at[pl.ds(r0, rn), pl.ds(c0, cn)],
            dst_ref=xe.at[pl.ds(to, rn), pl.ds(TO_COLS[dx], cn)],
            send_sem=near_send.at[n],
            recv_sem=near_recv.at[n],
            device_id=(la + dy, lax.rem(lo + dx + nlon, nlon)),
            device_id_type=MESH,
        )

    def each_near(act, sign, first, last):
        for n in range(first, min(last, 4)):
            act(near(n))
        if last > 4:
            for dy in (-1, 1):

                @pl.when(there(sign * dy))
                def _():
                    for n in range(4, 10):
                        if NEAR[n][0] == dy:
                            act(near(n))

    each_near(lambda c: c.start(), 1, 0, 10)
    for n in (POL, CM, COFF, G1, G2, EOFF, MIX, EMAT, KMAT):
        local[n].start()

    @pl.when(north)
    def _():
        xe[0:EDGE_ROWS] = jnp.zeros((EDGE_ROWS, WIDE, VARS), bf16)

    @pl.when(south)
    def _():
        xe[TALL - EDGE_ROWS : TALL] = jnp.zeros((EDGE_ROWS, WIDE, VARS), bf16)

    nv[EXT_ROWS] = jnp.zeros((EXT_COLS, FEAT), bf16)

    for n in (FOOT, CKE, NK):
        local[n].wait()
    chosen = jnp.where(
        lax.broadcasted_iota(jnp.int32, (EXT_COLS, total), 0) + la * ROWS - 1
        == lax.broadcasted_iota(jnp.int32, (EXT_COLS, total), 1),
        1.0,
        0.0,
    ).astype(bf16)
    for k in range(BASIS):
        entries = lax.dot_general(
            chosen, ckev[k], (((1,), (1,)), ((), ())), preferred_element_type=f32
        )
        entv[:, k, :] = entries[:EXT_ROWS]
    cycle = lax.broadcasted_iota(jnp.int32, (CELLS, total), 1)
    place = lax.broadcasted_iota(jnp.int32, (CELLS, 256), 1).astype(f32)

    @pl.loop(0, EXT_ROWS)
    def _(i):
        cells = footv[...]
        lanes = (cells + (WINDOW - LWIN) * ((cells * 205) >> 11) + 6).astype(f32)
        column = jnp.sum(
            jnp.where(cycle == la * ROWS + i - 1, lanes, 0.0), axis=1, keepdims=True
        )
        onehot = jnp.where(column == place, 1.0, 0.0).astype(bf16)
        dense = jnp.dot(entv[i].astype(bf16), onehot, preferred_element_type=f32)
        w[i] = jnp.concatenate(
            [toeplitz(dense[k : k + 1], GROUP, 0, 2) for k in range(BASIS)], axis=0
        ).astype(bf16)

    def local_filters():
        s = lax.broadcasted_iota(jnp.int32, (RLOC * LLOC, 128), 0)
        lane = lax.broadcasted_iota(jnp.int32, (RLOC * LLOC, 128), 1)
        spread = jnp.where(
            ((lane & 31) < LLOC) & ((lane >> 5) * LLOC + (lane & 31) == s), 1.0, 0.0
        ).astype(bf16)
        for k in range(BASIS):
            tapv[k] = jnp.dot(nkv[k], spread, preferred_element_type=f32)

        @pl.loop(0, ROWS)
        def _(i):
            b[i] = jnp.concatenate(
                [toeplitz(tapv[k, pl.ds(i, 1), :], COLS, 0, 1) for k in range(BASIS)], axis=0
            ).astype(bf16)

    local[CM].wait()
    for k in range(BASIS):
        cmp[k * 128 : k * 128 + VARS, :] = cmv[k * VARS : (k + 1) * VARS, :]
        cmp[k * 128 + VARS : (k + 1) * 128, :] = jnp.zeros((128 - VARS, FEAT), bf16)

    @pl.when(jnp.logical_not(polar))
    def _():
        local[POL].wait()
        local_filters()

    for n in (COFF, G1, OWN):
        local[n].wait()

    first = jnp.where(upper, 1, ROWS - 3)
    offset = coffv[...].reshape(1, FEAT)
    gain = g1v[...].reshape(1, FEAT)

    def coarsen(begin, count):
        parts = []
        for m in range(count):
            i = lax.rem(begin + m, EXT_ROWS)
            rows = xe[pl.ds(2 * i, RIN)]
            windows = [
                jnp.concatenate(
                    [
                        rows[:, 16 * a : 16 * a + WINDOW, :].reshape(RIN * WINDOW, VARS),
                        jnp.zeros((RIN * WINDOW, 128 - VARS), bf16),
                    ],
                    axis=1,
                )
                for a in range(EXT_COLS // GROUP)
            ]
            windows = jnp.concatenate(windows, axis=1)
            windows = jnp.concatenate(
                [windows, jnp.zeros((256 - RIN * WINDOW, windows.shape[1]), bf16)], axis=0
            )
            got = jnp.dot(w[i], windows, preferred_element_type=f32)
            for a in range(EXT_COLS // GROUP):
                parts.append(
                    jnp.concatenate(
                        [
                            got[k * GROUP : (k + 1) * GROUP, a * 128 : (a + 1) * 128]
                            for k in range(BASIS)
                        ],
                        axis=1,
                    )
                )
        latent = jnp.dot(
            jnp.concatenate(parts, axis=0).astype(bf16), cmp[...], preferred_element_type=f32
        )
        latent = (latent + offset).astype(bf16).astype(f32)
        normed = norm(latent, gain)
        for m in range(count):
            i = lax.rem(begin + m, EXT_ROWS)
            g = la * ROWS + i - 1
            lat[i] = latent[m * EXT_COLS : (m + 1) * EXT_COLS]
            row = normed[m * EXT_COLS : (m + 1) * EXT_COLS]
            nv[i] = jnp.where((g >= 0) & (g < total), row, 0.0).astype(bf16)
        return normed

    def cap(m):
        return pltpu.make_async_remote_copy(
            src_ref=gath.at[0],
            dst_ref=gath.at[nlon - 2 * m],
            send_sem=cap_send.at[m - 1],
            recv_sem=cap_recv.at[m - 1],
            device_id=(la, lax.rem(lo + 2 * m, nlon)),
            device_id_type=MESH,
        )

    def hand(m, out=True):
        slot = (nlon - 2 * m) % nlon
        west = jnp.where(core == 0, nlon - 1, 1) if out else jnp.where(core == 0, 1, nlon - 1)
        return pltpu.make_async_remote_copy(
            src_ref=gath.at[slot],
            dst_ref=gath.at[lax.rem(slot + west, nlon)],
            send_sem=hand_send.at[m],
            recv_sem=hand_recv.at[m],
            device_id=(la, sibling),
            device_id_type=MESH,
        )

    def pass_on(ms):
        for m in ms:
            cap(m).wait_recv()
            hand(m).start()

    each_near(lambda c: c.wait_recv(), -1, 0, 2)

    @pl.when(jnp.logical_not(polar))
    def _():
        each_near(lambda c: c.wait_recv(), -1, 2, 10)

    normed = coarsen(first, 4)

    @pl.when(polar)
    def _():
        rows = [normed[m * EXT_COLS + 3 : m * EXT_COLS + 3 + COLS] for m in range(4)]
        gath[0] = jnp.concatenate(rows, axis=0).astype(bf16)
        for m in range(1, chips):
            cap(m).start()
        hand(0).start()
        each_near(lambda c: c.wait_recv(), -1, 2, 10)

    span = nlon * SLOT

    @pl.when(polar)
    def _():
        local[POL].wait()
        lane = lax.broadcasted_iota(jnp.int32, (1, span), 1)
        dev = lane // SLOT
        inner = lane - dev * SLOT
        cycle = inner // COLS
        inner = inner - cycle * COLS
        source = jnp.where(cycle == 0, dev * COLS + inner, -1)
        pick = jnp.where(
            lax.broadcasted_iota(jnp.int32, (nlon * COLS, span), 0) == source, 1.0, 0.0
        ).astype(bf16)
        lead = jnp.where(north, 1, 0)
        polf[...] = jnp.zeros(polf.shape, f32)
        for t in range(CAP):
            for r in range(RLOC):
                for k in range(BASIS):
                    both = polv[t, k, r].astype(f32)
                    n = (t * RLOC + r) * 16 + k
                    polf[n : n + 1, :] = jnp.where(north, both[0:1], both[1:2])
        poltaps[...] = jnp.dot(polf[...].astype(bf16), pick, preferred_element_type=f32)
        for t in range(CAP):
            line = jnp.zeros((16, span), f32)
            for r in range(RLOC):
                n = (t * RLOC + r) * 16
                to = t + r - lead
                moved = pltpu.roll(poltaps[n : n + 16, :], lax.rem(COLS * to + span, span), 1)
                line = line + jnp.where(cycle == to, moved, 0.0)
            lines[t * 16 : (t + 1) * 16, :] = line
        inside = inner >= lax.broadcasted_iota(jnp.int32, (COLS, span), 0)

        def circulant(n):
            t = n // BASIS
            line = lines[pl.ds(t * 16 + n - t * BASIS, 1), :]
            return jnp.where(
                inside, toeplitz(line, COLS, 0, 1), toeplitz(line, COLS, SLOT - COLS, 1)
            )

        @pl.loop(0, (CAP * BASIS + 1) // 2)
        def _(n):
            both = jnp.concatenate(
                [circulant(2 * n), circulant(jnp.minimum(2 * n + 1, CAP * BASIS - 1))], axis=0
            )
            lhs[pl.ds(pl.multiple_of(2 * COLS * n, 2 * COLS), 2 * COLS), :] = both.astype(bf16)

    def coarsen_rest():
        @pl.loop(0, 2)
        def _(n):
            coarsen(first + 4 + 7 * n, 7)

    def filters(i, extra):
        rhs = nv[pl.ds(i, 4)].reshape(4 * EXT_COLS, FEAT)
        got = jnp.dot(b[i], rhs, preferred_element_type=f32)
        return got if extra is None else got + extra

    def filter_pair(i, extra=None):
        one = filters(i, None if extra is None else pres[extra])
        two = filters(i + 1, None if extra is None else pres[extra + 1])
        for k in range(BASIS):
            both = jnp.concatenate(
                [one[k * COLS : (k + 1) * COLS], two[k * COLS : (k + 1) * COLS]], axis=0
            )
            filt[
                pl.ds(pl.multiple_of(i * COLS, 2 * COLS), 2 * COLS), k * FEAT : (k + 1) * FEAT
            ] = both.astype(bf16)

    expand_offset = eoffv
    gain_two = g2v

    def finish(i, rows):
        at = pl.ds(pl.multiple_of(i * COLS, 2 * COLS), rows * COLS)
        residual = lat[pl.ds(i + 1, rows), 3 : 3 + COLS, :].reshape(rows * COLS, FEAT)
        middle = residual + jnp.dot(filt[at, :], mixv[...], preferred_element_type=f32)
        middle = middle.astype(bf16).astype(f32)
        normed = norm(middle, gain_two[...].reshape(1, FEAT)).astype(bf16)
        hidden = jnp.dot(normed, ematv[...], preferred_element_type=f32)
        hidden = gelu(hidden + expand_offset[...].reshape(1, HIDDEN)).astype(bf16)
        encoded = middle + jnp.dot(hidden, kmatv[...], preferred_element_type=f32)
        outv[at, :] = encoded.astype(bf16)

    def store(part, i, rows):
        at = pl.ds(pl.multiple_of(i * COLS, 2 * COLS), rows * COLS)
        return pltpu.make_async_copy(outv.at[at], out.at[at], out_sem.at[part])

    @pl.when(jnp.logical_not(polar))
    def _():
        coarsen_rest()

        @pl.loop(0, ROWS // 2)
        def _(n):
            filter_pair(2 * n)

        for n in (G2, EOFF, MIX, EMAT, KMAT):
            local[n].wait()
        finish(0, ROWS)
        copy = store(0, 0, ROWS)
        copy.start()
        copy.wait()

    @pl.when(polar)
    def _():
        big, small = jnp.where(north, 4, 0), jnp.where(north, 0, ROWS - 4)
        near_by = sorted({1, chips - 1, chips // 2} - {0})
        rest = [m for m in range(1, chips) if m not in near_by]
        some = len(rest) // 2
        local_filters()
        coarsen_rest()
        @pl.loop(0, (ROWS - 4) // 2)
        def _(n):
            filter_pair(big + 2 * n)

        pass_on(near_by)
        pass_on(rest)
        for n in (G2, EOFF, MIX, EMAT, KMAT):
            local[n].wait()
        finish(big, 12)
        store(0, big, 6).start()
        store(1, big + 6, 6).start()
        for m in range(chips):
            hand(m, False).wait_recv()
        got = jnp.dot(lhs[...], gath[...].reshape(span, FEAT), preferred_element_type=f32)
        lead = jnp.where(north, 0, 1)
        pres[jnp.where(north, 3, 0)] = jnp.zeros((BASIS * COLS, FEAT), f32)
        for t in range(CAP):
            pres[t + lead] = got[t * BASIS * COLS : (t + 1) * BASIS * COLS]
        filter_pair(small, 0)
        filter_pair(small + 2, 2)
        finish(small, 4)
        store(2, small, 4).start()
        for m in range(1, chips):
            cap(m).wait_send()
        for m in range(chips):
            hand(m).wait_send()
        store(0, big, 6).wait()
        store(1, big + 6, 6).wait()
        store(2, small, 4).wait()

    each_near(lambda c: c.wait_send(), 1, 0, 10)


def copy_kernel(source, out, sem):
    rows = source.shape[0] // 4
    parts = [
        pltpu.make_async_copy(
            source.at[pl.ds(n * rows, rows)], out.at[pl.ds(n * rows, rows)], sem.at[n]
        )
        for n in range(4)
    ]
    for part in parts:
        part.start()
    for part in parts:
        part.wait()


def body(x, foot, cke, cmat, coff, g1, nk, pol, mix, g2, emat, eoff, kmat):
    nlat, nlon = lax.axis_size("lat"), lax.axis_size("lon")
    span = nlon * SLOT
    vmem = pltpu.VMEM
    scratch = [
        vmem((TALL, WIDE, VARS), bf16),
        vmem((CELLS, nlat * ROWS), jnp.int32),
        vmem((BASIS, CELLS, nlat * ROWS), bf16),
        vmem((BASIS * VARS, FEAT), bf16),
        vmem((FEAT,), f32),
        vmem((FEAT,), f32),
        vmem((BASIS, ROWS, RLOC * LLOC), bf16),
        vmem((CAP, BASIS, RLOC, 2, nlon * COLS), bf16),
        vmem((BASIS * FEAT, FEAT), bf16),
        vmem((FEAT,), f32),
        vmem((FEAT, HIDDEN), bf16),
        vmem((HIDDEN,), f32),
        vmem((HIDDEN, FEAT), bf16),
        vmem((EXT_ROWS, BASIS, CELLS), f32),
        vmem((BASIS, ROWS, 128), f32),
        vmem((CAP * RLOC * 16, nlon * COLS), f32),
        vmem((CAP * RLOC * 16, span), f32),
        vmem((CAP * 16, span), f32),
        vmem((BASIS * 128, FEAT), bf16),
        vmem((EXT_ROWS, BASIS * GROUP, 256), bf16),
        vmem((ROWS, BASIS * COLS, 128), bf16),
        vmem((EXT_ROWS + 1, EXT_COLS, FEAT), bf16),
        vmem((EXT_ROWS, EXT_COLS, FEAT), f32),
        vmem((ROWS * COLS, BASIS * FEAT), bf16),
        vmem((nlon, SLOT, FEAT), bf16),
        vmem(((CAP * BASIS + 1) * COLS, span), bf16),
        vmem((4, BASIS * COLS, FEAT), f32),
        vmem((ROWS * COLS, FEAT), bf16),
        pltpu.SemaphoreType.DMA((13,)),
        pltpu.SemaphoreType.DMA((10,)),
        pltpu.SemaphoreType.DMA((10,)),
        pltpu.SemaphoreType.DMA((nlon // 2 - 1,)),
        pltpu.SemaphoreType.DMA((nlon // 2 - 1,)),
        pltpu.SemaphoreType.DMA((nlon // 2,)),
        pltpu.SemaphoreType.DMA((nlon // 2,)),
        pltpu.SemaphoreType.DMA((3,)),
    ]
    encoded = pl.pallas_call(
        functools.partial(kernel, nlat, nlon),
        out_shape=jax.ShapeDtypeStruct((ROWS * COLS, FEAT), bf16),
        in_specs=[pl.BlockSpec(memory_space=pl.ANY)] * 13,
        out_specs=pl.BlockSpec(memory_space=pl.ANY),
        scratch_shapes=scratch,
        compiler_params=pltpu.CompilerParams(
            collective_id=0, has_side_effects=True, vmem_limit_bytes=56 << 20
        ),
        cost_estimate=pl.CostEstimate(
            flops=3_000_000_000, bytes_accessed=9_000_000, transcendentals=400_000
        ),
    )(
        x,
        foot.T,
        cke.transpose(1, 2, 0),
        cmat,
        coff,
        g1,
        nk.transpose(1, 0, 2),
        pol.transpose(1, 2, 3, 0, 4),
        mix,
        g2,
        emat,
        eoff,
        kmat,
    )
    return encoded.reshape(ROWS, COLS, FEAT)


def solution(mesh):
    return jax.shard_map(
        body,
        mesh=mesh,
        in_specs=(
            P("lat", "lon", None),
            P(),
            P(),
            P(),
            P(),
            P(),
            P("lat", None, None),
            P(),
            P(),
            P(),
            P(),
            P(),
            P(),
        ),
        out_specs=P("lat", "lon", None),
        check_vma=False,
    )
```

```python
import functools

import jax
import jax.numpy as jnp
from jax import lax
from jax.experimental import pallas as pl
from jax.experimental.pallas import tpu as pltpu
from jax.sharding import PartitionSpec as P

VARS = 72
FEAT = 512
HIDDEN = 1024
BASIS = 9
RIN = 6
LWIN = 10
CELLS = 32
RLOC = 3
LLOC = 7
CAP = 3
ROWS = 16
COLS = 24
IN_ROWS = 2 * ROWS
IN_COLS = 2 * COLS
EDGE_ROWS = 4
EDGE_COLS = 16
WIDE = EDGE_COLS + IN_COLS + EDGE_COLS
TALL = EDGE_ROWS + IN_ROWS + EDGE_ROWS
EXT_ROWS = ROWS + 2
EXT_COLS = 32
SLOT = 4 * COLS
INNER = 20
FRONT = 4 * INNER
QUAD = 4 * COLS
PAD_ROWS = 224
EPS = 1e-05
bf16, f32 = jnp.bfloat16, jnp.float32
MESH = pl.DeviceIdType.MESH

EARLY = 12
NEAR = [(0, -1), (0, 1), (0, -1), (0, 1)] + [(dy, dx) for dy in (-1, 1) for dx in (-1, 0, 1)]
FROM_ROWS = {-1: 0, 1: IN_ROWS - EDGE_ROWS}
TO_ROWS = {-1: EDGE_ROWS + IN_ROWS, 1: 0}
FROM_COLS = {-1: (0, EDGE_COLS), 0: (0, IN_COLS), 1: (IN_COLS - EDGE_COLS, EDGE_COLS)}
TO_COLS = {-1: EDGE_COLS + IN_COLS, 0: EDGE_COLS, 1: 0}
GROUP = 8
WINDOW = 32


def norm(wide, gain):
    center = jnp.mean(wide, axis=-1, keepdims=True)
    off = wide - center
    spread = jnp.mean(off * off, axis=-1, keepdims=True)
    return off * lax.rsqrt(spread + EPS) * gain


def gelu(u):
    return 0.5 * u * (1.0 + jnp.tanh(0.7978845608 * (u + 0.044715 * (u * u * u))))


def toeplitz(row, count, shift, stride):
    return pltpu.roll(
        jnp.broadcast_to(row, (count, row.shape[1])), shift, 1, stride=stride, stride_axis=0
    )


def kernel(
    nlat, nlon,
    x, foot, cke, cmat, coff, g1, nk, pol, mix, g2, emat, eoff, kmat,
    out,
    xe, footv, ckev, cmv, coffv, g1v, nkv, polv, mixv, g2v, ematv, eoffv, kmatv,
    entv, tapv, polf, sort, taps, cmp, w, b, nv, lat, filt, gath, lhs, pres,
    local_sem, near_send, near_recv, cap_send, cap_recv, hand_send, hand_recv,
):
    la, lo = lax.axis_index("lat"), lax.axis_index("lon")
    north = la == 0
    south = la == nlat - 1
    polar = north | south
    upper = la < nlat // 2
    total = nlat * ROWS
    chips = nlon // 2
    core = lax.rem(lo, 2)
    sibling = lo + 1 - 2 * core

    barrier = pltpu.get_barrier_semaphore()

    def there(dy):
        return (la + dy >= 0) & (la + dy < nlat)

    def greet(dy, dx):
        pl.semaphore_signal(
            barrier, inc=1, device_id=(la + dy, lax.rem(lo + dx + nlon, nlon)), device_id_type=MESH
        )

    for dy in (-1, 1):
        @pl.when(there(dy))
        def _():
            for dx in (-1, 0, 1):
                greet(dy, dx)

    greet(0, -1)
    greet(0, 1)

    @pl.when(polar)
    def _():
        for m in range(1, chips):
            greet(0, 2 * m)

    pairs = [
        (foot, footv),
        (cke, ckev),
        (nk, nkv),
        (x, xe.at[pl.ds(EDGE_ROWS, IN_ROWS), pl.ds(EDGE_COLS, IN_COLS)]),
        (cmat, cmv),
        (coff, coffv),
        (g1, g1v),
        (pol, polv),
        (g2, g2v),
        (eoff, eoffv),
        (mix, mixv),
        (emat, ematv),
        (kmat, kmatv),
    ]
    FOOT, CKE, NK, OWN, CM, COFF, G1, POL, G2, EOFF, MIX, EMAT, KMAT = range(13)
    local = [pltpu.make_async_copy(s, d, local_sem.at[n]) for n, (s, d) in enumerate(pairs)]
    for n in (FOOT, CKE, OWN, CM, COFF, G1, NK, POL):
        local[n].start()

    pl.semaphore_wait(
        barrier,
        2 + jnp.where(polar, chips - 1, 0) + jnp.where(north, 0, 3) + jnp.where(south, 0, 3),
    )

    def near(n):
        dy, dx = NEAR[n]
        c0, cn = FROM_COLS[dx]
        if n < 2:
            r0, rn = jnp.where(upper, 0, IN_ROWS - EARLY), EARLY
            to = r0 + EDGE_ROWS
        elif n < 4:
            r0, rn = jnp.where(upper, EARLY, 0), IN_ROWS - EARLY
            to = r0 + EDGE_ROWS
        else:
            r0, rn, to = FROM_ROWS[dy], EDGE_ROWS, TO_ROWS[dy]
        return pltpu.make_async_remote_copy(
            src_ref=x.at[pl.ds(r0, rn), pl.ds(c0, cn)],
            dst_ref=xe.at[pl.ds(to, rn), pl.ds(TO_COLS[dx], cn)],
            send_sem=near_send.at[n],
            recv_sem=near_recv.at[n],
            device_id=(la + dy, lax.rem(lo + dx + nlon, nlon)),
            device_id_type=MESH,
        )

    def each_near(act, sign, first, last):
        for n in range(first, min(last, 4)):
            act(near(n))
        if last > 4:
            for dy in (-1, 1):

                @pl.when(there(sign * dy))
                def _():
                    for n in range(4, 10):
                        if NEAR[n][0] == dy:
                            act(near(n))

    each_near(lambda c: c.start(), 1, 0, 10)
    for n in (G2, EOFF, MIX, EMAT, KMAT):
        local[n].start()

    @pl.when(north)
    def _():
        xe[0:EDGE_ROWS] = jnp.zeros((EDGE_ROWS, WIDE, VARS), bf16)

    @pl.when(south)
    def _():
        xe[TALL - EDGE_ROWS : TALL] = jnp.zeros((EDGE_ROWS, WIDE, VARS), bf16)

    nv[EXT_ROWS] = jnp.zeros((EXT_COLS, FEAT), bf16)

    for n in (FOOT, CKE, NK):
        local[n].wait()
    chosen = jnp.where(
        lax.broadcasted_iota(jnp.int32, (EXT_COLS, total), 0) + la * ROWS - 1
        == lax.broadcasted_iota(jnp.int32, (EXT_COLS, total), 1),
        1.0,
        0.0,
    ).astype(bf16)
    for k in range(BASIS):
        entries = lax.dot_general(
            chosen, ckev[k], (((1,), (1,)), ((), ())), preferred_element_type=f32
        )
        entv[:, k, :] = entries[:EXT_ROWS]
    cycle = lax.broadcasted_iota(jnp.int32, (CELLS, total), 1)
    place = lax.broadcasted_iota(jnp.int32, (CELLS, 256), 1).astype(f32)

    first = jnp.where(upper, 1, ROWS - 3)

    def banded(n):
        i = lax.rem(first + n, EXT_ROWS)
        cells = footv[...]
        lanes = (cells + (WINDOW - LWIN) * ((cells * 205) >> 11) + 6).astype(f32)
        column = jnp.sum(
            jnp.where(cycle == la * ROWS + i - 1, lanes, 0.0), axis=1, keepdims=True
        )
        onehot = jnp.where(column == place, 1.0, 0.0).astype(bf16)
        dense = jnp.dot(entv[i].astype(bf16), onehot, preferred_element_type=f32)
        w[i] = jnp.concatenate(
            [toeplitz(dense[k : k + 1], GROUP, 0, 2) for k in range(BASIS)], axis=0
        ).astype(bf16)

    pl.loop(0, 4)(banded)

    def local_filters():
        s = lax.broadcasted_iota(jnp.int32, (RLOC * LLOC, 128), 0)
        lane = lax.broadcasted_iota(jnp.int32, (RLOC * LLOC, 128), 1)
        spread = jnp.where(
            ((lane & 31) < LLOC) & ((lane >> 5) * LLOC + (lane & 31) == s), 1.0, 0.0
        ).astype(bf16)
        for k in range(BASIS):
            tapv[k] = jnp.dot(nkv[k], spread, preferred_element_type=f32)

        @pl.loop(0, ROWS)
        def _(i):
            b[i] = jnp.concatenate(
                [toeplitz(tapv[k, pl.ds(i, 1), :], COLS, 0, 1) for k in range(BASIS)], axis=0
            ).astype(bf16)

    local[CM].wait()
    for k in range(BASIS):
        cmp[k * 128 : k * 128 + VARS, :] = cmv[k * VARS : (k + 1) * VARS, :]
        cmp[k * 128 + VARS : (k + 1) * 128, :] = jnp.zeros((128 - VARS, FEAT), bf16)

    for n in (COFF, G1, OWN, POL):
        local[n].wait()

    offset = coffv[...].reshape(1, FEAT)
    gain = g1v[...].reshape(1, FEAT)

    def coarsen(begin, count, sides=True):
        parts = []
        for m in range(count):
            i = lax.rem(begin + m, EXT_ROWS)
            if sides:
                rows = xe[pl.ds(2 * i, RIN)]
            else:
                none = jnp.zeros((RIN, EDGE_COLS, VARS), bf16)
                own = xe[pl.ds(2 * i, RIN), EDGE_COLS : EDGE_COLS + IN_COLS]
                rows = jnp.concatenate([none, own, none], axis=1)
            windows = [
                jnp.concatenate(
                    [
                        rows[:, 16 * a : 16 * a + WINDOW, :].reshape(RIN * WINDOW, VARS),
                        jnp.zeros((RIN * WINDOW, 128 - VARS), bf16),
                    ],
                    axis=1,
                )
                for a in range(EXT_COLS // GROUP)
            ]
            windows = jnp.concatenate(windows, axis=1)
            windows = jnp.concatenate(
                [windows, jnp.zeros((256 - RIN * WINDOW, windows.shape[1]), bf16)], axis=0
            )
            got = jnp.dot(w[i], windows, preferred_element_type=f32)
            for a in range(EXT_COLS // GROUP):
                parts.append(
                    jnp.concatenate(
                        [
                            got[k * GROUP : (k + 1) * GROUP, a * 128 : (a + 1) * 128]
                            for k in range(BASIS)
                        ],
                        axis=1,
                    )
                )
        latent = jnp.dot(
            jnp.concatenate(parts, axis=0).astype(bf16), cmp[...], preferred_element_type=f32
        )
        latent = (latent + offset).astype(bf16).astype(f32)
        normed = norm(latent, gain)
        if not sides:
            return normed
        for m in range(count):
            i = lax.rem(begin + m, EXT_ROWS)
            g = la * ROWS + i - 1
            lat[i] = latent[m * EXT_COLS : (m + 1) * EXT_COLS]
            row = normed[m * EXT_COLS : (m + 1) * EXT_COLS]
            nv[i] = jnp.where((g >= 0) & (g < total), row, 0.0).astype(bf16)
        return normed

    def cap(m, late):
        at = pl.ds(FRONT, SLOT - FRONT) if late else pl.ds(0, FRONT)
        return pltpu.make_async_remote_copy(
            src_ref=gath.at[0, at],
            dst_ref=gath.at[nlon - 2 * m, at],
            send_sem=cap_send.at[late, m - 1],
            recv_sem=cap_recv.at[late, m - 1],
            device_id=(la, lax.rem(lo + 2 * m, nlon)),
            device_id_type=MESH,
        )

    def hand(m, out=True):
        slot = (nlon - 2 * m) % nlon
        west = jnp.where(core == 0, nlon - 1, 1) if out else jnp.where(core == 0, 1, nlon - 1)
        return pltpu.make_async_remote_copy(
            src_ref=gath.at[slot],
            dst_ref=gath.at[lax.rem(slot + west, nlon)],
            send_sem=hand_send.at[m],
            recv_sem=hand_recv.at[m],
            device_id=(la, sibling),
            device_id_type=MESH,
        )

    def pass_on(ms):
        for m in ms:
            cap(m, 0).wait_recv()
            cap(m, 1).wait_recv()
            hand(m).start()

    @pl.when(polar)
    def _():
        normed = coarsen(first, 4, False)
        rows = [normed[m * EXT_COLS + 5 : m * EXT_COLS + 5 + INNER] for m in range(4)]
        gath[0, 0:FRONT] = jnp.concatenate(rows, axis=0).astype(bf16)
        for m in (2, 6, 3, 5, 1, 7, 4):
            cap(m, 0).start()

    pl.loop(4, EXT_ROWS)(banded)

    quads = nlon // 4
    span = nlon * SLOT

    def polar_taps():
        lane = lax.broadcasted_iota(jnp.int32, (1, 4 * SLOT), 1)
        dev = lane // SLOT
        place = lane - dev * SLOT
        front = place < FRONT
        side = place - FRONT
        cycle = jnp.where(front, place // INNER, side // 4)
        end = side - 4 * (side // 4)
        inner = jnp.where(
            front, place - cycle * INNER + 2, jnp.where(end < 2, end, end + INNER)
        )
        lead = jnp.where(north, 1, 0)
        for t in range(CAP):
            r = cycle - t + lead
            source = jnp.where(
                (r >= 0) & (r < RLOC), r * 128 + dev * COLS + inner, -1
            )
            sort[t] = jnp.where(
                lax.broadcasted_iota(jnp.int32, (RLOC * 128, 4 * SLOT), 0) == source, 1.0, 0.0
            ).astype(bf16)
        polf[...] = jnp.zeros(polf.shape, f32)
        for t in range(CAP):
            for r in range(RLOC):
                for k in range(BASIS):
                    both = polv[t, k, r].astype(f32)
                    n = (t * RLOC + r) * 16 + k
                    polf[n : n + 1, :] = jnp.where(north, both[0:1], both[1:2])
        at = lax.broadcasted_iota(jnp.int32, (16, 128), 1)
        length = nlon * COLS
        for n in range(CAP * RLOC):
            line = polf[n * 16 : (n + 1) * 16, :]
            for q in range(quads):
                ahead = pltpu.roll(line, (length - QUAD * q) % length, 1)[:, :128]
                before = pltpu.roll(line, (length + 128 - QUAD * q) % length, 1)[:, :128]
                taps[n, q] = jnp.where(
                    at < QUAD, ahead, jnp.where(at >= 128 - COLS, before, 0.0)
                )

    def circulants():
        @pl.loop(0, quads)
        def _(q):
            for t in range(CAP):
                rows = []
                for k in range(BASIS):
                    rows.append(
                        jnp.concatenate(
                            [
                                toeplitz(taps[t * RLOC + r, q, k : k + 1, :], COLS, 0, 1)
                                for r in range(RLOC)
                            ],
                            axis=1,
                        )
                    )
                block = jnp.dot(
                    jnp.concatenate(rows, axis=0).astype(bf16),
                    sort[t],
                    preferred_element_type=f32,
                )
                lhs[
                    t * PAD_ROWS : t * PAD_ROWS + BASIS * COLS,
                    pl.ds(pl.multiple_of(4 * SLOT * q, 128), 4 * SLOT),
                ] = block.astype(bf16)

    @pl.when(jnp.logical_not(polar))
    def _():
        local_filters()

    @pl.when(polar)
    def _():
        polar_taps()

    each_near(lambda c: c.wait_recv(), -1, 0, 2)

    @pl.when(polar)
    def _():
        normed = coarsen(first, 4)
        rows = []
        for m in range(4):
            rows.append(normed[m * EXT_COLS + 3 : m * EXT_COLS + 5])
            rows.append(normed[m * EXT_COLS + 5 + INNER : m * EXT_COLS + 7 + INNER])
        gath[0, FRONT:SLOT] = jnp.concatenate(rows, axis=0).astype(bf16)
        for m in (2, 6, 3, 5, 1, 7, 4):
            cap(m, 1).start()
        hand(0).start()

    def filters(i, extra):
        rhs = nv[pl.ds(i, 4)].reshape(4 * EXT_COLS, FEAT)
        got = jnp.dot(b[i], rhs, preferred_element_type=f32)
        return got if extra is None else got + extra

    def filter_pair(i, extra=None):
        one = filters(i, None if extra is None else pres[extra])
        two = filters(i + 1, None if extra is None else pres[extra + 1])
        for k in range(BASIS):
            both = jnp.concatenate(
                [one[k * COLS : (k + 1) * COLS], two[k * COLS : (k + 1) * COLS]], axis=0
            )
            filt[
                pl.ds(pl.multiple_of(i * COLS, 2 * COLS), 2 * COLS), k * FEAT : (k + 1) * FEAT
            ] = both.astype(bf16)

    expand_offset = eoffv
    gain_two = g2v

    def finish(i, rows):
        at = pl.ds(pl.multiple_of(i * COLS, 2 * COLS), rows * COLS)
        residual = lat[pl.ds(i + 1, rows), 3 : 3 + COLS, :].reshape(rows * COLS, FEAT)
        middle = residual + jnp.dot(filt[at, :], mixv[...], preferred_element_type=f32)
        middle = middle.astype(bf16).astype(f32)
        normed = norm(middle, gain_two[...].reshape(1, FEAT)).astype(bf16)
        hidden = jnp.dot(normed, ematv[...], preferred_element_type=f32)
        hidden = gelu(hidden + expand_offset[...].reshape(1, HIDDEN)).astype(bf16)
        encoded = middle + jnp.dot(hidden, kmatv[...], preferred_element_type=f32)
        out[at, :] = encoded.astype(bf16)

    @pl.when(jnp.logical_not(polar))
    def _():
        each_near(lambda c: c.wait_recv(), -1, 2, 4)

        @pl.loop(0, 2)
        def _(n):
            coarsen(2 + 7 * n, 7)

        each_near(lambda c: c.wait_recv(), -1, 4, 10)
        coarsen(ROWS, 4)

        @pl.loop(0, ROWS // 2)
        def _(n):
            filter_pair(2 * n)

        for n in (G2, EOFF, MIX, EMAT, KMAT):
            local[n].wait()
        finish(0, ROWS)

    @pl.when(polar)
    def _():
        big, small = jnp.where(north, 4, 0), jnp.where(north, 0, ROWS - 4)
        circulants()
        local_filters()
        each_near(lambda c: c.wait_recv(), -1, 2, 10)

        @pl.loop(0, 2)
        def _(n):
            coarsen(first + 4 + 7 * n, 7)

        @pl.loop(0, (ROWS - 4) // 2)
        def _(n):
            filter_pair(big + 2 * n)

        pass_on(range(1, chips))
        for n in (G2, EOFF, MIX, EMAT, KMAT):
            local[n].wait()
        finish(big, ROWS - 4)

        for m in range(chips):
            hand(m, False).wait_recv()
        got = jnp.dot(lhs[...], gath[...].reshape(span, FEAT), preferred_element_type=f32)
        lead = jnp.where(north, 0, 1)
        pres[jnp.where(north, 3, 0)] = jnp.zeros((BASIS * COLS, FEAT), f32)
        for t in range(CAP):
            pres[t + lead] = got[t * PAD_ROWS : t * PAD_ROWS + BASIS * COLS]
        filter_pair(small, 0)
        filter_pair(small + 2, 2)
        finish(small, 4)
        for m in range(1, chips):
            cap(m, 0).wait_send()
            cap(m, 1).wait_send()
        for m in range(chips):
            hand(m).wait_send()

    each_near(lambda c: c.wait_send(), 1, 0, 10)


def body(x, foot, cke, cmat, coff, g1, nk, pol, mix, g2, emat, eoff, kmat):
    nlat, nlon = lax.axis_size("lat"), lax.axis_size("lon")
    span = nlon * SLOT
    vmem = pltpu.VMEM
    scratch = [
        vmem((TALL, WIDE, VARS), bf16),
        vmem((CELLS, nlat * ROWS), jnp.int32),
        vmem((BASIS, CELLS, nlat * ROWS), bf16),
        vmem((BASIS * VARS, FEAT), bf16),
        vmem((FEAT,), f32),
        vmem((FEAT,), f32),
        vmem((BASIS, ROWS, RLOC * LLOC), bf16),
        vmem((CAP, BASIS, RLOC, 2, nlon * COLS), bf16),
        vmem((BASIS * FEAT, FEAT), bf16),
        vmem((FEAT,), f32),
        vmem((FEAT, HIDDEN), bf16),
        vmem((HIDDEN,), f32),
        vmem((HIDDEN, FEAT), bf16),
        vmem((EXT_ROWS, BASIS, CELLS), f32),
        vmem((BASIS, ROWS, 128), f32),
        vmem((CAP * RLOC * 16, nlon * COLS), f32),
        vmem((CAP, RLOC * 128, 4 * SLOT), bf16),
        vmem((CAP * RLOC, nlon // 4, 16, 128), f32),
        vmem((BASIS * 128, FEAT), bf16),
        vmem((EXT_ROWS, BASIS * GROUP, 256), bf16),
        vmem((ROWS, BASIS * COLS, 128), bf16),
        vmem((EXT_ROWS + 1, EXT_COLS, FEAT), bf16),
        vmem((EXT_ROWS, EXT_COLS, FEAT), f32),
        vmem((ROWS * COLS, BASIS * FEAT), bf16),
        vmem((nlon, SLOT, FEAT), bf16),
        vmem((CAP * PAD_ROWS, span), bf16),
        vmem((4, BASIS * COLS, FEAT), f32),
        pltpu.SemaphoreType.DMA((13,)),
        pltpu.SemaphoreType.DMA((10,)),
        pltpu.SemaphoreType.DMA((10,)),
        pltpu.SemaphoreType.DMA((2, nlon // 2 - 1)),
        pltpu.SemaphoreType.DMA((2, nlon // 2 - 1)),
        pltpu.SemaphoreType.DMA((nlon // 2,)),
        pltpu.SemaphoreType.DMA((nlon // 2,)),
    ]
    encoded = pl.pallas_call(
        functools.partial(kernel, nlat, nlon),
        out_shape=pltpu.VMEM((ROWS * COLS, FEAT), bf16),
        in_specs=[pl.BlockSpec(memory_space=pl.ANY)] * 13,
        out_specs=pl.BlockSpec(memory_space=pltpu.VMEM),
        scratch_shapes=scratch,
        compiler_params=pltpu.CompilerParams(
            collective_id=0, has_side_effects=True, vmem_limit_bytes=56 << 20
        ),
        cost_estimate=pl.CostEstimate(
            flops=3_000_000_000, bytes_accessed=9_000_000, transcendentals=400_000
        ),
    )(
        x,
        foot.T,
        cke.transpose(1, 2, 0),
        cmat,
        coff,
        g1,
        nk.transpose(1, 0, 2),
        pol.transpose(1, 2, 3, 0, 4),
        mix,
        g2,
        emat,
        eoff,
        kmat,
    )
    return encoded.reshape(ROWS, COLS, FEAT)


def solution(mesh):
    return jax.shard_map(
        body,
        mesh=mesh,
        in_specs=(
            P("lat", "lon", None),
            P(),
            P(),
            P(),
            P(),
            P(),
            P("lat", None, None),
            P(),
            P(),
            P(),
            P(),
            P(),
            P(),
        ),
        out_specs=P("lat", "lon", None),
        check_vma=False,
    )
```

```python
import functools

import jax
import jax.numpy as jnp
from jax import lax
from jax.experimental import pallas as pl
from jax.experimental.pallas import tpu as pltpu
from jax.sharding import PartitionSpec as P

VARS = 72
FEAT = 512
HIDDEN = 1024
BASIS = 9
RIN = 6
LWIN = 10
CELLS = 32
RLOC = 3
LLOC = 7
CAP = 3
ROWS = 16
COLS = 24
IN_ROWS = 2 * ROWS
IN_COLS = 2 * COLS
EDGE_ROWS = 4
EDGE_COLS = 16
WIDE = EDGE_COLS + IN_COLS + EDGE_COLS
TALL = EDGE_ROWS + IN_ROWS + EDGE_ROWS
EXT_ROWS = ROWS + 2
EXT_COLS = 32
SLOT = 4 * COLS
INNER = 20
FRONT = 4 * INNER
QUAD = 4 * COLS
PAD_ROWS = 224
EPS = 1e-05
bf16, f32 = jnp.bfloat16, jnp.float32
MESH = pl.DeviceIdType.MESH

EARLY = 12
NEAR = [(0, -1), (0, 1), (0, -1), (0, 1)] + [(dy, dx) for dy in (-1, 1) for dx in (-1, 0, 1)]
FROM_ROWS = {-1: 0, 1: IN_ROWS - EDGE_ROWS}
TO_ROWS = {-1: EDGE_ROWS + IN_ROWS, 1: 0}
FROM_COLS = {-1: (0, EDGE_COLS), 0: (0, IN_COLS), 1: (IN_COLS - EDGE_COLS, EDGE_COLS)}
TO_COLS = {-1: EDGE_COLS + IN_COLS, 0: EDGE_COLS, 1: 0}
GROUP = 8
WINDOW = 32


def norm(wide, gain):
    center = jnp.mean(wide, axis=-1, keepdims=True)
    off = wide - center
    spread = jnp.mean(off * off, axis=-1, keepdims=True)
    return off * lax.rsqrt(spread + EPS) * gain


def gelu(u):
    return 0.5 * u * (1.0 + jnp.tanh(0.7978845608 * (u + 0.044715 * (u * u * u))))


def toeplitz(row, count, shift, stride):
    return pltpu.roll(
        jnp.broadcast_to(row, (count, row.shape[1])), shift, 1, stride=stride, stride_axis=0
    )


def kernel(
    nlat, nlon,
    x, foot, cke, cmat, coff, g1, nk, pol, mix, g2, emat, eoff, kmat,
    out,
    xe, footv, ckev, cmv, coffv, g1v, nkv, polv, mixv, g2v, ematv, eoffv, kmatv,
    entv, tapv, polf, sort, taps, cmp, w, b, nv, lat, filt, gath, lhs, pres,
    local_sem, near_send, near_recv, cap_send, cap_recv, hand_send, hand_recv,
):
    la, lo = lax.axis_index("lat"), lax.axis_index("lon")
    north = la == 0
    south = la == nlat - 1
    polar = north | south
    upper = la < nlat // 2
    total = nlat * ROWS
    chips = nlon // 2
    core = lax.rem(lo, 2)
    sibling = lo + 1 - 2 * core

    barrier = pltpu.get_barrier_semaphore()

    def there(dy):
        return (la + dy >= 0) & (la + dy < nlat)

    def greet(dy, dx):
        pl.semaphore_signal(
            barrier, inc=1, device_id=(la + dy, lax.rem(lo + dx + nlon, nlon)), device_id_type=MESH
        )

    for dy in (-1, 1):
        @pl.when(there(dy))
        def _():
            for dx in (-1, 0, 1):
                greet(dy, dx)

    greet(0, -1)
    greet(0, 1)

    @pl.when(polar)
    def _():
        for m in range(1, chips):
            greet(0, 2 * m)

    pairs = [
        (foot, footv),
        (cke, ckev),
        (nk, nkv),
        (x, xe.at[pl.ds(EDGE_ROWS, IN_ROWS), pl.ds(EDGE_COLS, IN_COLS)]),
        (cmat, cmv),
        (coff, coffv),
        (g1, g1v),
        (pol, polv),
        (g2, g2v),
        (eoff, eoffv),
        (mix, mixv),
        (emat, ematv),
        (kmat, kmatv),
    ]
    FOOT, CKE, NK, OWN, CM, COFF, G1, POL, G2, EOFF, MIX, EMAT, KMAT = range(13)
    local = [pltpu.make_async_copy(s, d, local_sem.at[n]) for n, (s, d) in enumerate(pairs)]
    for n in (FOOT, CKE, OWN, CM, COFF, G1, NK, POL):
        local[n].start()

    def near(n):
        dy, dx = NEAR[n]
        c0, cn = FROM_COLS[dx]
        if n < 2:
            r0, rn = jnp.where(upper, 0, IN_ROWS - EARLY), EARLY
            to = r0 + EDGE_ROWS
        elif n < 4:
            r0, rn = jnp.where(upper, EARLY, 0), IN_ROWS - EARLY
            to = r0 + EDGE_ROWS
        else:
            r0, rn, to = FROM_ROWS[dy], EDGE_ROWS, TO_ROWS[dy]
        return pltpu.make_async_remote_copy(
            src_ref=x.at[pl.ds(r0, rn), pl.ds(c0, cn)],
            dst_ref=xe.at[pl.ds(to, rn), pl.ds(TO_COLS[dx], cn)],
            send_sem=near_send.at[n],
            recv_sem=near_recv.at[n],
            device_id=(la + dy, lax.rem(lo + dx + nlon, nlon)),
            device_id_type=MESH,
        )

    def each_near(act, sign, first, last):
        for n in range(first, min(last, 4)):
            act(near(n))
        if last > 4:
            for dy in (-1, 1):

                @pl.when(there(sign * dy))
                def _():
                    for n in range(4, 10):
                        if NEAR[n][0] == dy:
                            act(near(n))

    @pl.when(north)
    def _():
        xe[0:EDGE_ROWS] = jnp.zeros((EDGE_ROWS, WIDE, VARS), bf16)

    @pl.when(south)
    def _():
        xe[TALL - EDGE_ROWS : TALL] = jnp.zeros((EDGE_ROWS, WIDE, VARS), bf16)

    nv[EXT_ROWS] = jnp.zeros((EXT_COLS, FEAT), bf16)

    for n in (FOOT, CKE, NK):
        local[n].wait()
    chosen = jnp.where(
        lax.broadcasted_iota(jnp.int32, (EXT_COLS, total), 0) + la * ROWS - 1
        == lax.broadcasted_iota(jnp.int32, (EXT_COLS, total), 1),
        1.0,
        0.0,
    ).astype(bf16)
    for k in range(BASIS):
        entries = lax.dot_general(
            chosen, ckev[k], (((1,), (1,)), ((), ())), preferred_element_type=f32
        )
        entv[:, k, :] = entries[:EXT_ROWS]
    cycle = lax.broadcasted_iota(jnp.int32, (CELLS, total), 1)
    place = lax.broadcasted_iota(jnp.int32, (CELLS, 256), 1).astype(f32)

    first = jnp.where(upper, 1, ROWS - 3)

    def banded(n):
        i = lax.rem(first + n, EXT_ROWS)
        cells = footv[...]
        lanes = (cells + (WINDOW - LWIN) * ((cells * 205) >> 11) + 6).astype(f32)
        column = jnp.sum(
            jnp.where(cycle == la * ROWS + i - 1, lanes, 0.0), axis=1, keepdims=True
        )
        onehot = jnp.where(column == place, 1.0, 0.0).astype(bf16)
        dense = jnp.dot(entv[i].astype(bf16), onehot, preferred_element_type=f32)
        w[i] = jnp.concatenate(
            [toeplitz(dense[k : k + 1], GROUP, 0, 2) for k in range(BASIS)], axis=0
        ).astype(bf16)

    pl.loop(0, 4, unroll=4)(banded)

    def local_filters():
        s = lax.broadcasted_iota(jnp.int32, (RLOC * LLOC, 128), 0)
        lane = lax.broadcasted_iota(jnp.int32, (RLOC * LLOC, 128), 1)
        spread = jnp.where(
            ((lane & 31) < LLOC) & ((lane >> 5) * LLOC + (lane & 31) == s), 1.0, 0.0
        ).astype(bf16)
        for k in range(BASIS):
            tapv[k] = jnp.dot(nkv[k], spread, preferred_element_type=f32)

        @pl.loop(0, ROWS, unroll=4)
        def _(i):
            b[i] = jnp.concatenate(
                [toeplitz(tapv[k, pl.ds(i, 1), :], COLS, 0, 1) for k in range(BASIS)], axis=0
            ).astype(bf16)

    local[CM].wait()
    for k in range(BASIS):
        cmp[k * 128 : k * 128 + VARS, :] = cmv[k * VARS : (k + 1) * VARS, :]
        cmp[k * 128 + VARS : (k + 1) * 128, :] = jnp.zeros((128 - VARS, FEAT), bf16)

    for n in (COFF, G1, OWN, POL):
        local[n].wait()

    offset = coffv[...].reshape(1, FEAT)
    gain = g1v[...].reshape(1, FEAT)

    def coarsen(begin, count, sides=True):
        parts = []
        for m in range(count):
            i = lax.rem(begin + m, EXT_ROWS)
            if sides:
                rows = xe[pl.ds(2 * i, RIN)]
            else:
                none = jnp.zeros((RIN, EDGE_COLS, VARS), bf16)
                own = xe[pl.ds(2 * i, RIN), EDGE_COLS : EDGE_COLS + IN_COLS]
                rows = jnp.concatenate([none, own, none], axis=1)
            windows = [
                jnp.concatenate(
                    [
                        rows[:, 16 * a : 16 * a + WINDOW, :].reshape(RIN * WINDOW, VARS),
                        jnp.zeros((RIN * WINDOW, 128 - VARS), bf16),
                    ],
                    axis=1,
                )
                for a in range(EXT_COLS // GROUP)
            ]
            windows = jnp.concatenate(windows, axis=1)
            windows = jnp.concatenate(
                [windows, jnp.zeros((256 - RIN * WINDOW, windows.shape[1]), bf16)], axis=0
            )
            got = jnp.dot(w[i], windows, preferred_element_type=f32)
            for a in range(EXT_COLS // GROUP):
                parts.append(
                    jnp.concatenate(
                        [
                            got[k * GROUP : (k + 1) * GROUP, a * 128 : (a + 1) * 128]
                            for k in range(BASIS)
                        ],
                        axis=1,
                    )
                )
        latent = jnp.dot(
            jnp.concatenate(parts, axis=0).astype(bf16), cmp[...], preferred_element_type=f32
        )
        latent = (latent + offset).astype(bf16).astype(f32)
        normed = norm(latent, gain)
        if not sides:
            return normed
        for m in range(count):
            i = lax.rem(begin + m, EXT_ROWS)
            g = la * ROWS + i - 1
            lat[i] = latent[m * EXT_COLS : (m + 1) * EXT_COLS]
            row = normed[m * EXT_COLS : (m + 1) * EXT_COLS]
            nv[i] = jnp.where((g >= 0) & (g < total), row, 0.0).astype(bf16)
        return normed

    sending = sorted(range(1, chips), key=lambda m: (abs(abs(2 * m - chips) - chips // 2), m))

    def part(late):
        return pl.ds(FRONT, SLOT - FRONT) if late else pl.ds(0, FRONT)

    def cap(m, late):
        at = part(late)
        return pltpu.make_async_remote_copy(
            src_ref=gath.at[0, at],
            dst_ref=gath.at[nlon - 2 * m, at],
            send_sem=cap_send.at[late, m - 1],
            recv_sem=cap_recv.at[late, m - 1],
            device_id=(la, lax.rem(lo + 2 * m, nlon)),
            device_id_type=MESH,
        )

    def hand(m, late, out=True):
        slot = (nlon - 2 * m) % nlon
        west = jnp.where(core == 0, nlon - 1, 1) if out else jnp.where(core == 0, 1, nlon - 1)
        return pltpu.make_async_remote_copy(
            src_ref=gath.at[slot, part(late)],
            dst_ref=gath.at[lax.rem(slot + west, nlon), part(late)],
            send_sem=hand_send.at[late, m],
            recv_sem=hand_recv.at[late, m],
            device_id=(la, sibling),
            device_id_type=MESH,
        )

    def pass_on(late):
        for m in sending:
            cap(m, late).wait_recv()
            hand(m, late).start()

    @pl.when(polar)
    def _():
        normed = coarsen(first, 4, False)
        rows = [normed[m * EXT_COLS + 5 : m * EXT_COLS + 5 + INNER] for m in range(4)]
        gath[0, 0:FRONT] = jnp.concatenate(rows, axis=0).astype(bf16)

    pl.semaphore_wait(
        barrier,
        2 + jnp.where(polar, chips - 1, 0) + jnp.where(north, 0, 3) + jnp.where(south, 0, 3),
    )

    each_near(lambda c: c.start(), 1, 0, 10)
    @pl.when(polar)
    def _():
        for m in sending:
            cap(m, 0).start()

    for n in (G2, EOFF, MIX, EMAT, KMAT):
        local[n].start()

    pl.loop(4, EXT_ROWS, unroll=7)(banded)

    quads = nlon // 4
    span = nlon * SLOT

    def polar_taps():
        lane = lax.broadcasted_iota(jnp.int32, (1, 4 * SLOT), 1)
        dev = lane // SLOT
        place = lane - dev * SLOT
        front = place < FRONT
        side = place - FRONT
        cycle = jnp.where(front, place // INNER, side // 4)
        end = side - 4 * (side // 4)
        inner = jnp.where(
            front, place - cycle * INNER + 2, jnp.where(end < 2, end, end + INNER)
        )
        lead = jnp.where(north, 1, 0)
        for t in range(CAP):
            r = cycle - t + lead
            source = jnp.where(
                (r >= 0) & (r < RLOC), r * 128 + dev * COLS + inner, -1
            )
            sort[t] = jnp.where(
                lax.broadcasted_iota(jnp.int32, (RLOC * 128, 4 * SLOT), 0) == source, 1.0, 0.0
            ).astype(bf16)
        polf[...] = jnp.zeros(polf.shape, f32)
        for t in range(CAP):
            for r in range(RLOC):
                for k in range(BASIS):
                    both = polv[t, k, r].astype(f32)
                    n = (t * RLOC + r) * 16 + k
                    polf[n : n + 1, :] = jnp.where(north, both[0:1], both[1:2])
        at = lax.broadcasted_iota(jnp.int32, (16, 128), 1)
        length = nlon * COLS
        for n in range(CAP * RLOC):
            line = polf[n * 16 : (n + 1) * 16, :]
            for q in range(quads):
                ahead = pltpu.roll(line, (length - QUAD * q) % length, 1)[:, :128]
                before = pltpu.roll(line, (length + 128 - QUAD * q) % length, 1)[:, :128]
                taps[n, q] = jnp.where(
                    at < QUAD, ahead, jnp.where(at >= 128 - COLS, before, 0.0)
                )

    def circulants():
        @pl.loop(0, quads, unroll=4)
        def _(q):
            for t in range(CAP):
                rows = []
                for k in range(BASIS):
                    rows.append(
                        jnp.concatenate(
                            [
                                toeplitz(taps[t * RLOC + r, q, k : k + 1, :], COLS, 0, 1)
                                for r in range(RLOC)
                            ],
                            axis=1,
                        )
                    )
                block = jnp.dot(
                    jnp.concatenate(rows, axis=0).astype(bf16),
                    sort[t],
                    preferred_element_type=f32,
                )
                lhs[
                    t * PAD_ROWS : t * PAD_ROWS + BASIS * COLS,
                    pl.ds(pl.multiple_of(4 * SLOT * q, 128), 4 * SLOT),
                ] = block.astype(bf16)

    @pl.when(jnp.logical_not(polar))
    def _():
        local_filters()

    @pl.when(polar)
    def _():
        polar_taps()

    each_near(lambda c: c.wait_recv(), -1, 0, 2)

    @pl.when(polar)
    def _():
        normed = coarsen(first, 4)
        rows = []
        for m in range(4):
            rows.append(normed[m * EXT_COLS + 3 : m * EXT_COLS + 5])
            rows.append(normed[m * EXT_COLS + 5 + INNER : m * EXT_COLS + 7 + INNER])
        gath[0, FRONT:SLOT] = jnp.concatenate(rows, axis=0).astype(bf16)
        for m in sending:
            cap(m, 1).start()
        hand(0, 0).start()
        hand(0, 1).start()

    def filters(i, extra):
        rhs = nv[pl.ds(i, 4)].reshape(4 * EXT_COLS, FEAT)
        got = jnp.dot(b[i], rhs, preferred_element_type=f32)
        return got if extra is None else got + extra

    def filter_pair(i, extra=None):
        one = filters(i, None if extra is None else pres[extra])
        two = filters(i + 1, None if extra is None else pres[extra + 1])
        for k in range(BASIS):
            both = jnp.concatenate(
                [one[k * COLS : (k + 1) * COLS], two[k * COLS : (k + 1) * COLS]], axis=0
            )
            filt[
                pl.ds(pl.multiple_of(i * COLS, 2 * COLS), 2 * COLS), k * FEAT : (k + 1) * FEAT
            ] = both.astype(bf16)

    expand_offset = eoffv
    gain_two = g2v

    def finish(i, rows):
        at = pl.ds(pl.multiple_of(i * COLS, 2 * COLS), rows * COLS)
        residual = lat[pl.ds(i + 1, rows), 3 : 3 + COLS, :].reshape(rows * COLS, FEAT)
        middle = residual + jnp.dot(filt[at, :], mixv[...], preferred_element_type=f32)
        middle = middle.astype(bf16).astype(f32)
        normed = norm(middle, gain_two[...].reshape(1, FEAT)).astype(bf16)
        hidden = jnp.dot(normed, ematv[...], preferred_element_type=f32)
        hidden = gelu(hidden + expand_offset[...].reshape(1, HIDDEN)).astype(bf16)
        encoded = middle + jnp.dot(hidden, kmatv[...], preferred_element_type=f32)
        out[at, :] = encoded.astype(bf16)

    @pl.when(jnp.logical_not(polar))
    def _():
        each_near(lambda c: c.wait_recv(), -1, 2, 4)

        @pl.loop(0, 2)
        def _(n):
            coarsen(2 + 7 * n, 7)

        each_near(lambda c: c.wait_recv(), -1, 4, 10)
        coarsen(ROWS, 4)

        @pl.loop(0, ROWS // 2, unroll=2)
        def _(n):
            filter_pair(2 * n)

        for n in (G2, EOFF, MIX, EMAT, KMAT):
            local[n].wait()
        finish(0, ROWS)

    @pl.when(polar)
    def _():
        big, small = jnp.where(north, 4, 0), jnp.where(north, 0, ROWS - 4)
        circulants()
        local_filters()
        each_near(lambda c: c.wait_recv(), -1, 2, 10)

        @pl.loop(0, 2)
        def _(n):
            coarsen(first + 4 + 7 * n, 7)

        @pl.loop(0, (ROWS - 4) // 2, unroll=2)
        def _(n):
            filter_pair(big + 2 * n)

        for n in (G2, EOFF, MIX, EMAT, KMAT):
            local[n].wait()
        finish(big, 6)
        pass_on(0)
        pass_on(1)
        finish(big + 6, 6)

        for m in range(chips):
            hand(m, 0, False).wait_recv()
            hand(m, 1, False).wait_recv()
        got = jnp.dot(lhs[...], gath[...].reshape(span, FEAT), preferred_element_type=f32)
        lead = jnp.where(north, 0, 1)
        pres[jnp.where(north, 3, 0)] = jnp.zeros((BASIS * COLS, FEAT), f32)
        for t in range(CAP):
            pres[t + lead] = got[t * PAD_ROWS : t * PAD_ROWS + BASIS * COLS]
        filter_pair(small, 0)
        filter_pair(small + 2, 2)
        finish(small, 4)
        for m in range(1, chips):
            cap(m, 0).wait_send()
            cap(m, 1).wait_send()
        for m in range(chips):
            hand(m, 0).wait_send()
            hand(m, 1).wait_send()

    each_near(lambda c: c.wait_send(), 1, 0, 10)


def body(x, foot, cke, cmat, coff, g1, nk, pol, mix, g2, emat, eoff, kmat):
    nlat, nlon = lax.axis_size("lat"), lax.axis_size("lon")
    span = nlon * SLOT
    vmem = pltpu.VMEM
    scratch = [
        vmem((TALL, WIDE, VARS), bf16),
        vmem((CELLS, nlat * ROWS), jnp.int32),
        vmem((BASIS, CELLS, nlat * ROWS), bf16),
        vmem((BASIS * VARS, FEAT), bf16),
        vmem((FEAT,), f32),
        vmem((FEAT,), f32),
        vmem((BASIS, ROWS, RLOC * LLOC), bf16),
        vmem((CAP, BASIS, RLOC, 2, nlon * COLS), bf16),
        vmem((BASIS * FEAT, FEAT), bf16),
        vmem((FEAT,), f32),
        vmem((FEAT, HIDDEN), bf16),
        vmem((HIDDEN,), f32),
        vmem((HIDDEN, FEAT), bf16),
        vmem((EXT_ROWS, BASIS, CELLS), f32),
        vmem((BASIS, ROWS, 128), f32),
        vmem((CAP * RLOC * 16, nlon * COLS), f32),
        vmem((CAP, RLOC * 128, 4 * SLOT), bf16),
        vmem((CAP * RLOC, nlon // 4, 16, 128), f32),
        vmem((BASIS * 128, FEAT), bf16),
        vmem((EXT_ROWS, BASIS * GROUP, 256), bf16),
        vmem((ROWS, BASIS * COLS, 128), bf16),
        vmem((EXT_ROWS + 1, EXT_COLS, FEAT), bf16),
        vmem((EXT_ROWS, EXT_COLS, FEAT), f32),
        vmem((ROWS * COLS, BASIS * FEAT), bf16),
        vmem((nlon, SLOT, FEAT), bf16),
        vmem((CAP * PAD_ROWS, span), bf16),
        vmem((4, BASIS * COLS, FEAT), f32),
        pltpu.SemaphoreType.DMA((13,)),
        pltpu.SemaphoreType.DMA((10,)),
        pltpu.SemaphoreType.DMA((10,)),
        pltpu.SemaphoreType.DMA((2, nlon // 2 - 1)),
        pltpu.SemaphoreType.DMA((2, nlon // 2 - 1)),
        pltpu.SemaphoreType.DMA((2, nlon // 2)),
        pltpu.SemaphoreType.DMA((2, nlon // 2)),
    ]
    encoded = pl.pallas_call(
        functools.partial(kernel, nlat, nlon),
        out_shape=pltpu.VMEM((ROWS * COLS, FEAT), bf16),
        in_specs=[pl.BlockSpec(memory_space=pl.ANY)] * 13,
        out_specs=pl.BlockSpec(memory_space=pltpu.VMEM),
        scratch_shapes=scratch,
        compiler_params=pltpu.CompilerParams(
            collective_id=0, has_side_effects=True, vmem_limit_bytes=56 << 20
        ),
        cost_estimate=pl.CostEstimate(
            flops=3_000_000_000, bytes_accessed=9_000_000, transcendentals=400_000
        ),
    )(
        x,
        foot.T,
        cke.transpose(1, 2, 0),
        cmat,
        coff,
        g1,
        nk.transpose(1, 0, 2),
        pol.transpose(1, 2, 3, 0, 4),
        mix,
        g2,
        emat,
        eoff,
        kmat,
    )
    return encoded.reshape(ROWS, COLS, FEAT)


def solution(mesh):
    return jax.shard_map(
        body,
        mesh=mesh,
        in_specs=(
            P("lat", "lon", None),
            P(),
            P(),
            P(),
            P(),
            P(),
            P("lat", None, None),
            P(),
            P(),
            P(),
            P(),
            P(),
            P(),
        ),
        out_specs=P("lat", "lon", None),
        check_vma=False,
    )
```

```python
import functools

import jax
import jax.numpy as jnp
from jax import lax
from jax.experimental import pallas as pl
from jax.experimental.pallas import tpu as pltpu
from jax.sharding import PartitionSpec as P

VARS = 72
FEAT = 512
HIDDEN = 1024
BASIS = 9
RIN = 6
LWIN = 10
CELLS = 32
RLOC = 3
LLOC = 7
CAP = 3
ROWS = 16
COLS = 24
IN_ROWS = 2 * ROWS
IN_COLS = 2 * COLS
EDGE_ROWS = 4
EDGE_COLS = 16
WIDE = EDGE_COLS + IN_COLS + EDGE_COLS
TALL = EDGE_ROWS + IN_ROWS + EDGE_ROWS
EXT_ROWS = ROWS + 2
EXT_COLS = 32
SLOT = 4 * COLS
INNER = 20
FRONT = 4 * INNER
QUAD = 4 * COLS
PAD_ROWS = 224
EPS = 1e-05
bf16, f32 = jnp.bfloat16, jnp.float32
MESH = pl.DeviceIdType.MESH

EARLY = 12
NEAR = [(0, -1), (0, 1), (0, -1), (0, 1)] + [(dy, dx) for dy in (-1, 1) for dx in (-1, 0, 1)]
FROM_ROWS = {-1: 0, 1: IN_ROWS - EDGE_ROWS}
TO_ROWS = {-1: EDGE_ROWS + IN_ROWS, 1: 0}
FROM_COLS = {-1: (0, EDGE_COLS), 0: (0, IN_COLS), 1: (IN_COLS - EDGE_COLS, EDGE_COLS)}
TO_COLS = {-1: EDGE_COLS + IN_COLS, 0: EDGE_COLS, 1: 0}
GROUP = 8
WINDOW = 32


def norm(wide, gain):
    center = jnp.mean(wide, axis=-1, keepdims=True)
    off = wide - center
    spread = jnp.mean(off * off, axis=-1, keepdims=True)
    return off * lax.rsqrt(spread + EPS) * gain


def gelu(u):
    return 0.5 * u * (1.0 + jnp.tanh(0.7978845608 * (u + 0.044715 * (u * u * u))))


def toeplitz(row, count, shift, stride):
    return pltpu.roll(
        jnp.broadcast_to(row, (count, row.shape[1])), shift, 1, stride=stride, stride_axis=0
    )


def kernel(
    nlat, nlon,
    x, foot, cke, cmat, coff, g1, nk, pol, mix, g2, emat, eoff, kmat,
    out,
    xe, footv, ckev, cmv, coffv, g1v, nkv, polv, mixv, g2v, ematv, eoffv, kmatv,
    entv, tapv, polf, sort, taps, cmp, w, b, nv, lat, filt, gath, lhs, pres,
    local_sem, near_send, near_recv, cap_send, cap_recv, hand_send, hand_recv,
):
    la, lo = lax.axis_index("lat"), lax.axis_index("lon")
    north = la == 0
    south = la == nlat - 1
    polar = north | south
    upper = la < nlat // 2
    total = nlat * ROWS
    chips = nlon // 2
    core = lax.rem(lo, 2)
    sibling = lo + 1 - 2 * core

    barrier = pltpu.get_barrier_semaphore()

    def there(dy):
        return (la + dy >= 0) & (la + dy < nlat)

    def greet(dy, dx):
        pl.semaphore_signal(
            barrier, inc=1, device_id=(la + dy, lax.rem(lo + dx + nlon, nlon)), device_id_type=MESH
        )

    for dy in (-1, 1):
        @pl.when(there(dy))
        def _():
            for dx in (-1, 0, 1):
                greet(dy, dx)

    greet(0, -1)
    greet(0, 1)

    @pl.when(polar)
    def _():
        for m in range(1, chips):
            greet(0, 2 * m)

    pairs = [
        (foot, footv),
        (cke, ckev),
        (nk, nkv),
        (x, xe.at[pl.ds(EDGE_ROWS, IN_ROWS), pl.ds(EDGE_COLS, IN_COLS)]),
        (cmat, cmv),
        (coff, coffv),
        (g1, g1v),
        (pol, polv),
        (g2, g2v),
        (eoff, eoffv),
        (mix, mixv),
        (emat, ematv),
        (kmat, kmatv),
    ]
    FOOT, CKE, NK, OWN, CM, COFF, G1, POL, G2, EOFF, MIX, EMAT, KMAT = range(13)
    local = [pltpu.make_async_copy(s, d, local_sem.at[n]) for n, (s, d) in enumerate(pairs)]
    for n in (FOOT, CKE, OWN, CM, COFF, G1, NK, POL):
        local[n].start()

    def near(n):
        dy, dx = NEAR[n]
        c0, cn = FROM_COLS[dx]
        if n < 2:
            r0, rn = jnp.where(upper, 0, IN_ROWS - EARLY), EARLY
            to = r0 + EDGE_ROWS
        elif n < 4:
            r0, rn = jnp.where(upper, EARLY, 0), IN_ROWS - EARLY
            to = r0 + EDGE_ROWS
        else:
            r0, rn, to = FROM_ROWS[dy], EDGE_ROWS, TO_ROWS[dy]
        return pltpu.make_async_remote_copy(
            src_ref=x.at[pl.ds(r0, rn), pl.ds(c0, cn)],
            dst_ref=xe.at[pl.ds(to, rn), pl.ds(TO_COLS[dx], cn)],
            send_sem=near_send.at[n],
            recv_sem=near_recv.at[n],
            device_id=(la + dy, lax.rem(lo + dx + nlon, nlon)),
            device_id_type=MESH,
        )

    def each_near(act, sign, first, last):
        for n in range(first, min(last, 4)):
            act(near(n))
        if last > 4:
            for dy in (-1, 1):

                @pl.when(there(sign * dy))
                def _():
                    for n in range(4, 10):
                        if NEAR[n][0] == dy:
                            act(near(n))

    @pl.when(north)
    def _():
        xe[0:EDGE_ROWS] = jnp.zeros((EDGE_ROWS, WIDE, VARS), bf16)

    @pl.when(south)
    def _():
        xe[TALL - EDGE_ROWS : TALL] = jnp.zeros((EDGE_ROWS, WIDE, VARS), bf16)

    nv[EXT_ROWS] = jnp.zeros((EXT_COLS, FEAT), bf16)

    for n in (FOOT, CKE, NK):
        local[n].wait()
    chosen = jnp.where(
        lax.broadcasted_iota(jnp.int32, (EXT_COLS, total), 0) + la * ROWS - 1
        == lax.broadcasted_iota(jnp.int32, (EXT_COLS, total), 1),
        1.0,
        0.0,
    ).astype(bf16)
    for k in range(BASIS):
        entries = lax.dot_general(
            chosen, ckev[k], (((1,), (1,)), ((), ())), preferred_element_type=f32
        )
        entv[:, k, :] = entries[:EXT_ROWS]
    cycle = lax.broadcasted_iota(jnp.int32, (CELLS, total), 1)
    place = lax.broadcasted_iota(jnp.int32, (CELLS, 256), 1).astype(f32)

    first = jnp.where(upper, 1, ROWS - 3)

    def banded(n):
        i = lax.rem(first + n, EXT_ROWS)
        cells = footv[...]
        lanes = (cells + (WINDOW - LWIN) * ((cells * 205) >> 11) + 6).astype(f32)
        column = jnp.sum(
            jnp.where(cycle == la * ROWS + i - 1, lanes, 0.0), axis=1, keepdims=True
        )
        onehot = jnp.where(column == place, 1.0, 0.0).astype(bf16)
        dense = jnp.dot(entv[i].astype(bf16), onehot, preferred_element_type=f32)
        w[i] = jnp.concatenate(
            [toeplitz(dense[k : k + 1], GROUP, 0, 2) for k in range(BASIS)], axis=0
        ).astype(bf16)

    pl.loop(0, 4, unroll=4)(banded)

    def local_filters():
        s = lax.broadcasted_iota(jnp.int32, (RLOC * LLOC, 128), 0)
        lane = lax.broadcasted_iota(jnp.int32, (RLOC * LLOC, 128), 1)
        spread = jnp.where(
            ((lane & 31) < LLOC) & ((lane >> 5) * LLOC + (lane & 31) == s), 1.0, 0.0
        ).astype(bf16)
        for k in range(BASIS):
            tapv[k] = jnp.dot(nkv[k], spread, preferred_element_type=f32)

        @pl.loop(0, ROWS, unroll=4)
        def _(i):
            b[i] = jnp.concatenate(
                [toeplitz(tapv[k, pl.ds(i, 1), :], COLS, 0, 1) for k in range(BASIS)], axis=0
            ).astype(bf16)

    local[CM].wait()
    for k in range(BASIS):
        cmp[k * 128 : k * 128 + VARS, :] = cmv[k * VARS : (k + 1) * VARS, :]
        cmp[k * 128 + VARS : (k + 1) * 128, :] = jnp.zeros((128 - VARS, FEAT), bf16)

    for n in (COFF, G1, OWN, POL):
        local[n].wait()

    offset = coffv[...].reshape(1, FEAT)
    gain = g1v[...].reshape(1, FEAT)

    def coarsen(begin, count, sides=True):
        parts = []
        for m in range(count):
            i = lax.rem(begin + m, EXT_ROWS)
            if sides:
                rows = xe[pl.ds(2 * i, RIN)]
            else:
                none = jnp.zeros((RIN, EDGE_COLS, VARS), bf16)
                own = xe[pl.ds(2 * i, RIN), EDGE_COLS : EDGE_COLS + IN_COLS]
                rows = jnp.concatenate([none, own, none], axis=1)
            windows = [
                jnp.concatenate(
                    [
                        rows[:, 16 * a : 16 * a + WINDOW, :].reshape(RIN * WINDOW, VARS),
                        jnp.zeros((RIN * WINDOW, 128 - VARS), bf16),
                    ],
                    axis=1,
                )
                for a in range(EXT_COLS // GROUP)
            ]
            windows = jnp.concatenate(windows, axis=1)
            windows = jnp.concatenate(
                [windows, jnp.zeros((256 - RIN * WINDOW, windows.shape[1]), bf16)], axis=0
            )
            got = jnp.dot(w[i], windows, preferred_element_type=f32)
            for a in range(EXT_COLS // GROUP):
                parts.append(
                    jnp.concatenate(
                        [
                            got[k * GROUP : (k + 1) * GROUP, a * 128 : (a + 1) * 128]
                            for k in range(BASIS)
                        ],
                        axis=1,
                    )
                )
        latent = jnp.dot(
            jnp.concatenate(parts, axis=0).astype(bf16), cmp[...], preferred_element_type=f32
        )
        latent = (latent + offset).astype(bf16).astype(f32)
        normed = norm(latent, gain)
        if not sides:
            return normed
        for m in range(count):
            i = lax.rem(begin + m, EXT_ROWS)
            g = la * ROWS + i - 1
            lat[i] = latent[m * EXT_COLS : (m + 1) * EXT_COLS]
            row = normed[m * EXT_COLS : (m + 1) * EXT_COLS]
            nv[i] = jnp.where((g >= 0) & (g < total), row, 0.0).astype(bf16)
        return normed

    sending = sorted(range(1, chips), key=lambda m: (abs(abs(2 * m - chips) - chips // 2), m))

    def part(late):
        return pl.ds(FRONT, SLOT - FRONT) if late else pl.ds(0, FRONT)

    def cap(m, late):
        at = part(late)
        return pltpu.make_async_remote_copy(
            src_ref=gath.at[0, at],
            dst_ref=gath.at[nlon - 2 * m, at],
            send_sem=cap_send.at[late, m - 1],
            recv_sem=cap_recv.at[late, m - 1],
            device_id=(la, lax.rem(lo + 2 * m, nlon)),
            device_id_type=MESH,
        )

    def hand(m, late, out=True):
        slot = (nlon - 2 * m) % nlon
        west = jnp.where(core == 0, nlon - 1, 1) if out else jnp.where(core == 0, 1, nlon - 1)
        return pltpu.make_async_remote_copy(
            src_ref=gath.at[slot, part(late)],
            dst_ref=gath.at[lax.rem(slot + west, nlon), part(late)],
            send_sem=hand_send.at[late, m],
            recv_sem=hand_recv.at[late, m],
            device_id=(la, sibling),
            device_id_type=MESH,
        )

    def pass_on(late):
        for m in sending:
            cap(m, late).wait_recv()
            hand(m, late).start()

    @pl.when(polar)
    def _():
        normed = coarsen(first, 4, False)
        rows = [normed[m * EXT_COLS + 5 : m * EXT_COLS + 5 + INNER] for m in range(4)]
        gath[0, 0:FRONT] = jnp.concatenate(rows, axis=0).astype(bf16)

    pl.semaphore_wait(
        barrier,
        2 + jnp.where(polar, chips - 1, 0) + jnp.where(north, 0, 3) + jnp.where(south, 0, 3),
    )

    each_near(lambda c: c.start(), 1, 0, 10)
    @pl.when(polar)
    def _():
        for m in sending:
            cap(m, 0).start()

    for n in (G2, EOFF, MIX, EMAT, KMAT):
        local[n].start()

    pl.loop(4, EXT_ROWS, unroll=7)(banded)

    quads = nlon // 4
    span = nlon * SLOT

    def polar_taps():
        lane = lax.broadcasted_iota(jnp.int32, (1, 4 * SLOT), 1)
        dev = lane // SLOT
        place = lane - dev * SLOT
        dev = jnp.where(dev == 1, 2, jnp.where(dev == 2, 1, dev))
        front = place < FRONT
        side = place - FRONT
        cycle = jnp.where(front, place // INNER, side // 4)
        end = side - 4 * (side // 4)
        inner = jnp.where(
            front, place - cycle * INNER + 2, jnp.where(end < 2, end, end + INNER)
        )
        lead = jnp.where(north, 1, 0)
        for t in range(CAP):
            r = cycle - t + lead
            source = jnp.where(
                (r >= 0) & (r < RLOC), r * 128 + dev * COLS + inner, -1
            )
            sort[t] = jnp.where(
                lax.broadcasted_iota(jnp.int32, (RLOC * 128, 4 * SLOT), 0) == source, 1.0, 0.0
            ).astype(bf16)
        polf[...] = jnp.zeros(polf.shape, f32)
        for t in range(CAP):
            for r in range(RLOC):
                for k in range(BASIS):
                    both = polv[t, k, r].astype(f32)
                    n = (t * RLOC + r) * 16 + k
                    polf[n : n + 1, :] = jnp.where(north, both[0:1], both[1:2])
        at = lax.broadcasted_iota(jnp.int32, (16, 128), 1)
        length = nlon * COLS
        for n in range(CAP * RLOC):
            line = polf[n * 16 : (n + 1) * 16, :]
            for q in range(quads):
                ahead = pltpu.roll(line, (length - QUAD * q) % length, 1)[:, :128]
                before = pltpu.roll(line, (length + 128 - QUAD * q) % length, 1)[:, :128]
                taps[n, q] = jnp.where(
                    at < QUAD, ahead, jnp.where(at >= 128 - COLS, before, 0.0)
                )

    def circulants():
        for q in range(quads):
            for t in range(CAP):
                rows = []
                for k in range(BASIS):
                    rows.append(
                        jnp.concatenate(
                            [
                                toeplitz(taps[t * RLOC + r, q, k : k + 1, :], COLS, 0, 1)
                                for r in range(RLOC)
                            ],
                            axis=1,
                        )
                    )
                block = jnp.dot(
                    jnp.concatenate(rows, axis=0).astype(bf16),
                    sort[t],
                    preferred_element_type=f32,
                )
                block = block.astype(bf16)
                at = slice(t * PAD_ROWS, t * PAD_ROWS + BASIS * COLS)
                for odd in range(2):
                    lhs[odd, at, 2 * SLOT * q : 2 * SLOT * (q + 1)] = block[
                        :, 2 * SLOT * odd : 2 * SLOT * (odd + 1)
                    ]

    @pl.when(jnp.logical_not(polar))
    def _():
        local_filters()

    @pl.when(polar)
    def _():
        polar_taps()

    each_near(lambda c: c.wait_recv(), -1, 0, 2)

    @pl.when(polar)
    def _():
        normed = coarsen(first, 4)
        rows = []
        for m in range(4):
            rows.append(normed[m * EXT_COLS + 3 : m * EXT_COLS + 5])
            rows.append(normed[m * EXT_COLS + 5 + INNER : m * EXT_COLS + 7 + INNER])
        gath[0, FRONT:SLOT] = jnp.concatenate(rows, axis=0).astype(bf16)
        for m in sending:
            cap(m, 1).start()
        hand(0, 0).start()
        hand(0, 1).start()

    def filters(i, extra):
        rhs = nv[pl.ds(i, 4)].reshape(4 * EXT_COLS, FEAT)
        got = jnp.dot(b[i], rhs, preferred_element_type=f32)
        return got if extra is None else got + extra

    def filter_pair(i, extra=None):
        one = filters(i, None if extra is None else pres[extra])
        two = filters(i + 1, None if extra is None else pres[extra + 1])
        for k in range(BASIS):
            both = jnp.concatenate(
                [one[k * COLS : (k + 1) * COLS], two[k * COLS : (k + 1) * COLS]], axis=0
            )
            filt[
                pl.ds(pl.multiple_of(i * COLS, 2 * COLS), 2 * COLS), k * FEAT : (k + 1) * FEAT
            ] = both.astype(bf16)

    expand_offset = eoffv
    gain_two = g2v

    def finish(i, rows):
        at = pl.ds(pl.multiple_of(i * COLS, 2 * COLS), rows * COLS)
        residual = lat[pl.ds(i + 1, rows), 3 : 3 + COLS, :].reshape(rows * COLS, FEAT)
        middle = residual + jnp.dot(filt[at, :], mixv[...], preferred_element_type=f32)
        middle = middle.astype(bf16).astype(f32)
        normed = norm(middle, gain_two[...].reshape(1, FEAT)).astype(bf16)
        hidden = jnp.dot(normed, ematv[...], preferred_element_type=f32)
        hidden = gelu(hidden + expand_offset[...].reshape(1, HIDDEN)).astype(bf16)
        encoded = middle + jnp.dot(hidden, kmatv[...], preferred_element_type=f32)
        out[at, :] = encoded.astype(bf16)

    @pl.when(jnp.logical_not(polar))
    def _():
        each_near(lambda c: c.wait_recv(), -1, 2, 4)

        @pl.loop(0, 2)
        def _(n):
            coarsen(2 + 7 * n, 7)

        each_near(lambda c: c.wait_recv(), -1, 4, 10)
        coarsen(ROWS, 4)

        @pl.loop(0, ROWS // 2, unroll=2)
        def _(n):
            filter_pair(2 * n)

        for n in (G2, EOFF, MIX, EMAT, KMAT):
            local[n].wait()
        finish(0, ROWS)

    @pl.when(polar)
    def _():
        big, small = jnp.where(north, 4, 0), jnp.where(north, 0, ROWS - 4)
        circulants()
        local_filters()
        each_near(lambda c: c.wait_recv(), -1, 2, 10)

        @pl.loop(0, 2)
        def _(n):
            coarsen(first + 4 + 7 * n, 7)

        @pl.loop(0, (ROWS - 4) // 2, unroll=2)
        def _(n):
            filter_pair(big + 2 * n)

        for n in (G2, EOFF, MIX, EMAT, KMAT):
            local[n].wait()
        finish(big, 6)
        pass_on(0)
        pass_on(1)
        lead = jnp.where(north, 0, 1)

        def whole_cycles(odd):
            rows = jnp.concatenate([gath[n] for n in range(odd, nlon, 2)], axis=0)
            got = jnp.dot(lhs[odd], rows, preferred_element_type=f32)
            return [got[t * PAD_ROWS : t * PAD_ROWS + BASIS * COLS] for t in range(CAP)]

        pres[jnp.where(north, 3, 0)] = jnp.zeros((BASIS * COLS, FEAT), f32)
        for t, got in enumerate(whole_cycles(0)):
            pres[t + lead] = got
        finish(big + 6, 6)

        for m in range(chips):
            hand(m, 0, False).wait_recv()
            hand(m, 1, False).wait_recv()
        for t, got in enumerate(whole_cycles(1)):
            pres[t + lead] += got
        filter_pair(small, 0)
        filter_pair(small + 2, 2)
        finish(small, 4)
        for m in range(1, chips):
            cap(m, 0).wait_send()
            cap(m, 1).wait_send()
        for m in range(chips):
            hand(m, 0).wait_send()
            hand(m, 1).wait_send()

    each_near(lambda c: c.wait_send(), 1, 0, 10)


def body(x, foot, cke, cmat, coff, g1, nk, pol, mix, g2, emat, eoff, kmat):
    nlat, nlon = lax.axis_size("lat"), lax.axis_size("lon")
    span = nlon * SLOT
    vmem = pltpu.VMEM
    scratch = [
        vmem((TALL, WIDE, VARS), bf16),
        vmem((CELLS, nlat * ROWS), jnp.int32),
        vmem((BASIS, CELLS, nlat * ROWS), bf16),
        vmem((BASIS * VARS, FEAT), bf16),
        vmem((FEAT,), f32),
        vmem((FEAT,), f32),
        vmem((BASIS, ROWS, RLOC * LLOC), bf16),
        vmem((CAP, BASIS, RLOC, 2, nlon * COLS), bf16),
        vmem((BASIS * FEAT, FEAT), bf16),
        vmem((FEAT,), f32),
        vmem((FEAT, HIDDEN), bf16),
        vmem((HIDDEN,), f32),
        vmem((HIDDEN, FEAT), bf16),
        vmem((EXT_ROWS, BASIS, CELLS), f32),
        vmem((BASIS, ROWS, 128), f32),
        vmem((CAP * RLOC * 16, nlon * COLS), f32),
        vmem((CAP, RLOC * 128, 4 * SLOT), bf16),
        vmem((CAP * RLOC, nlon // 4, 16, 128), f32),
        vmem((BASIS * 128, FEAT), bf16),
        vmem((EXT_ROWS, BASIS * GROUP, 256), bf16),
        vmem((ROWS, BASIS * COLS, 128), bf16),
        vmem((EXT_ROWS + 1, EXT_COLS, FEAT), bf16),
        vmem((EXT_ROWS, EXT_COLS, FEAT), f32),
        vmem((ROWS * COLS, BASIS * FEAT), bf16),
        vmem((nlon, SLOT, FEAT), bf16),
        vmem((2, CAP * PAD_ROWS, span // 2), bf16),
        vmem((4, BASIS * COLS, FEAT), f32),
        pltpu.SemaphoreType.DMA((13,)),
        pltpu.SemaphoreType.DMA((10,)),
        pltpu.SemaphoreType.DMA((10,)),
        pltpu.SemaphoreType.DMA((2, nlon // 2 - 1)),
        pltpu.SemaphoreType.DMA((2, nlon // 2 - 1)),
        pltpu.SemaphoreType.DMA((2, nlon // 2)),
        pltpu.SemaphoreType.DMA((2, nlon // 2)),
    ]
    encoded = pl.pallas_call(
        functools.partial(kernel, nlat, nlon),
        out_shape=pltpu.VMEM((ROWS * COLS, FEAT), bf16),
        in_specs=[pl.BlockSpec(memory_space=pl.ANY)] * 13,
        out_specs=pl.BlockSpec(memory_space=pltpu.VMEM),
        scratch_shapes=scratch,
        compiler_params=pltpu.CompilerParams(
            collective_id=0, has_side_effects=True, vmem_limit_bytes=56 << 20
        ),
        cost_estimate=pl.CostEstimate(
            flops=3_000_000_000, bytes_accessed=9_000_000, transcendentals=400_000
        ),
    )(
        x,
        foot.T,
        cke.transpose(1, 2, 0),
        cmat,
        coff,
        g1,
        nk.transpose(1, 0, 2),
        pol.transpose(1, 2, 3, 0, 4),
        mix,
        g2,
        emat,
        eoff,
        kmat,
    )
    return encoded.reshape(ROWS, COLS, FEAT)


def solution(mesh):
    return jax.shard_map(
        body,
        mesh=mesh,
        in_specs=(
            P("lat", "lon", None),
            P(),
            P(),
            P(),
            P(),
            P(),
            P("lat", None, None),
            P(),
            P(),
            P(),
            P(),
            P(),
            P(),
        ),
        out_specs=P("lat", "lon", None),
        check_vma=False,
    )
```
